32 devices in a mesh: dp: 8 (over z, core), pos: 4 (over y, x).
Axes of the slice: x: 2, y: 2, z: 4, core: 2. Of those that a mesh axis runs over, the one named last changes fastest.
Arguments:
- features: bfloat16 [64, 128, 224], P(('dp', 'pos')), may hold values from -6 to 6
- counts: int32 [32], P(('dp', 'pos')), may hold values from 1 to 2, as said below
- channel_order: int32 [224], replicated, may hold values from 0 to 223, each once
Outputs:
- mean: float32 [128, 100], P('pos')
- covariance: float32 [128, 100, 100], P('pos')
The draws below stay inside these ranges and needn't reach their ends.
Inputs may be any that keep to these rules, and one draw needn't show every extreme that they name: `counts`: some device has all 2 slots live and some device only one.
All inputs are finite; a program needn't handle non-finite values.
Results may differ from the reference program's by a relative error of at most 0.0003.
Values may be sent and summed in bfloat16 or wider, within the bound.
No kernel may reach another device: no remote copies, remote signals or barrier semaphores. Data moves between devices by JAX's collectives and lax.ppermute only.
A program may use at most 128 MiB of HBM per device.

```python
import jax
import jax.numpy as jnp
from jax import lax

C = 224
CH = 100
IMG_DEV = 2
P_DEV = 32
P_SIZE = 128
IMAGES = 64
N_POS = 4


def draw_counts(key, part):
    owner_count = IMAGES // IMG_DEV
    first_key, second_key = jax.random.split(key)
    values = jax.random.randint(first_key, (owner_count,), 1, IMG_DEV + 1)
    picked = jax.random.randint(second_key, (), 0, owner_count)
    values = values.at[picked].set(IMG_DEV)
    values = values.at[(picked + 1) % owner_count].set(1)
    return values.astype(jnp.int32)


def levels(rng, shape, pieces, low, high):
    gain, own = 1.0, jax.random.fold_in(rng, 6)
    for dim, shards_of in pieces:
        steps = jnp.exp(jax.random.uniform(jax.random.fold_in(own, dim), (shards_of,), jnp.float32, low / len(pieces), high / len(pieces)))
        gain = gain * jnp.repeat(steps, shape[dim] // shards_of).reshape([-1 if axis == dim else 1 for axis in range(len(shape))])
    return gain


def scatter_about(own_key, dims, deviation, most, cuts=(), kind=jnp.bfloat16):
    level = levels(own_key, dims, cuts, -0.22, 0.18) if cuts else 1.0
    values = jax.random.normal(own_key, dims, jnp.float32) * deviation * level
    return jnp.minimum(jnp.maximum(values, -most), most).astype(kind)


def setup_inputs(seed: int = 0) -> dict:
    key_list = jax.random.split(jax.random.key(seed), 4)
    return {
        "features": scatter_about(key_list[0], (IMAGES, P_SIZE, C), 1.0, 6.0, ((0, 32),)),
        "counts": draw_counts(jax.random.fold_in(key_list[3], 71), 0),
        "channel_order": jax.random.permutation(key_list[2], C).astype(jnp.int32),
    }


def reference(features, counts, channel_order):
    kept = channel_order[:CH]
    slot_ids = jnp.arange(IMAGES, dtype=jnp.int32)
    live = ((slot_ids % IMG_DEV) < counts[slot_ids // IMG_DEV]).astype(jnp.float32)
    total = jnp.sum(counts).astype(jnp.float32)
    identity = jnp.eye(CH, dtype=jnp.float32)

    def one_block(block_id):
        begin_row = (block_id * P_DEV).astype(jnp.int32)
        block = lax.dynamic_slice_in_dim(features, begin_row, P_DEV, 1)
        samples = jnp.take(block, kept, axis=2).astype(jnp.float32) * live[:, None, None]
        block_mean = jnp.sum(samples, axis=0) / total
        centered = (samples - block_mean[None]) * live[:, None, None]
        sums = jnp.einsum("gpc,gpd->pcd", centered, centered, precision=lax.Precision.HIGHEST)
        return block_mean, sums / (total - 1.0) + 0.01 * identity

    means, covs = lax.map(one_block, jnp.arange(N_POS, dtype=jnp.int32))
    return means.reshape(P_SIZE, CH), covs.reshape(P_SIZE, CH, CH)
```

```python
import functools

import jax
import jax.numpy as jnp
from jax import lax
from jax.experimental import pallas as pl
from jax.experimental.pallas import tpu as pltpu
from jax.sharding import PartitionSpec as P

CH = 100
CORES = 2
LANES = 128
MIB = 1 << 20


def partner(n, step):
    if n & (n - 1) == 0:
        return [(i, i ^ step) for i in range(n)]
    return [(i, (i + step) % n) for i in range(n)]


def shift(index, n, step, sign):
    if n & (n - 1) == 0:
        return index ^ step
    return lax.rem(index + sign * step + n, n)


def select_kernel(groups, pos_dev, order_ref, counts_ref, features_ref, *out_refs):
    slots, channels, positions = features_ref.shape
    me = lax.axis_index("pos")
    order = order_ref[...].reshape(1, channels)[:, :LANES]
    lane = lax.broadcasted_iota(jnp.int32, (channels, LANES), 1)
    row = lax.broadcasted_iota(jnp.int32, (channels, LANES), 0)
    picker = jnp.where((row == order) & (lane < CH), 1.0, 0.0).astype(jnp.bfloat16)
    flag = lax.broadcasted_iota(jnp.int32, (positions, LANES), 1) == CH
    owned = counts_ref[0]
    scratch = out_refs[-1]
    for slot in range(slots):
        picked = lax.dot_general(
            features_ref[slot], picker, (((0,), (0,)), ((), ())), preferred_element_type=jnp.float32
        )
        picked = jnp.where(flag, 1.0, picked)
        live = jnp.where(slot < owned, 1.0, 0.0)
        scratch[slot] = picked * live
    for step in range(groups):
        begin = pl.multiple_of(shift(me, groups, step, 1) * pos_dev, pos_dev)
        for slot in range(slots):
            out_refs[step][pl.ds(slot * pos_dev, pos_dev), :] = scratch[
                slot, pl.ds(begin, pos_dev), :
            ].astype(jnp.bfloat16)


def merge_kernel(slots, pos_dev, *refs):
    *in_refs, out_ref, scratch = refs
    images = len(in_refs) * slots
    for source, ref in enumerate(in_refs):
        block = ref[...].astype(jnp.float32)
        for slot in range(slots):
            scratch[pl.ds(source * slots + slot, pos_dev, stride=images), :] = block[
                slot * pos_dev : (slot + 1) * pos_dev
            ]
    out_ref[...] = scratch[...].astype(jnp.bfloat16)


def stats_kernel(images, rows, depth, *refs):
    *in_refs, mean_ref, cov_ref, held = refs
    blocks = len(in_refs)
    me = lax.axis_index("dp")
    for step, ref in enumerate(in_refs):
        z_step, c_step = step // CORES, step % CORES
        owner = shift(me // CORES, depth, z_step, -1) * CORES + ((me % CORES) ^ c_step)
        held[owner] = ref[...].astype(jnp.float32).reshape(rows, images, LANES)
    everyone = blocks * images
    live = jnp.broadcast_to(
        held[:, 0].reshape(everyone, LANES)[:, CH : CH + 1], (everyone, LANES)
    )
    total = jnp.sum(live, axis=0, keepdims=True)
    factor = 1.0 / (total - 1.0)
    eye = lax.broadcasted_iota(jnp.int32, (LANES, LANES), 0) == lax.broadcasted_iota(
        jnp.int32, (LANES, LANES), 1
    )
    ridge = jnp.where(eye, 0.01, 0.0)
    for position in range(rows):
        samples = held[:, position].reshape(everyone, LANES)
        mean = jnp.sum(samples, axis=0, keepdims=True) / total
        mean_ref[pl.ds(position, 1), :] = mean[:, :CH]
        centered = samples - mean * live
        high = centered.astype(jnp.bfloat16)
        low = (centered - high.astype(jnp.float32)).astype(jnp.bfloat16)
        sums = lax.dot_general(
            jnp.concatenate([high, high, low], axis=0),
            jnp.concatenate([high, low, high], axis=0),
            (((0,), (0,)), ((), ())),
            preferred_element_type=jnp.float32,
        )
        cov_ref[:, position, :] = (sums * factor + ridge)[:CH, :CH]


def on_device(features, counts, channel_order):
    slots, positions, channels = features.shape
    groups, dp = lax.axis_size("pos"), lax.axis_size("dp")
    depth = dp // CORES
    pos_dev = positions // groups
    images = groups * slots
    wire = jnp.bfloat16
    vmem = pl.BlockSpec(memory_space=pltpu.VMEM)

    parts = pl.pallas_call(
        functools.partial(select_kernel, groups, pos_dev),
        out_shape=[jax.ShapeDtypeStruct((slots * pos_dev, LANES), wire)] * groups,
        in_specs=[vmem, pl.BlockSpec(memory_space=pltpu.SMEM), vmem],
        out_specs=[vmem] * groups,
        scratch_shapes=[pltpu.VMEM((slots, positions, LANES), jnp.float32)],
        compiler_params=pltpu.CompilerParams(vmem_limit_bytes=16 * MIB),
    )(channel_order, counts, jnp.transpose(features, (0, 2, 1)))

    got = [parts[0]] + [
        lax.ppermute(parts[step], "pos", partner(groups, step)) for step in range(1, groups)
    ]

    own = pl.pallas_call(
        functools.partial(merge_kernel, slots, pos_dev),
        out_shape=jax.ShapeDtypeStruct((pos_dev * images, LANES), wire),
        in_specs=[vmem] * groups,
        out_specs=vmem,
        scratch_shapes=[pltpu.VMEM((pos_dev * images, LANES), jnp.float32)],
        compiler_params=pltpu.CompilerParams(vmem_limit_bytes=16 * MIB),
    )(*got)

    blocks = {}
    swap = [(i, i ^ 1) for i in range(dp)]
    order = sorted(range(1, depth), reverse=True)
    blocks[0] = own
    for step in order:
        pairs = [
            (a * CORES + c, b * CORES + c) for a, b in partner(depth, step) for c in range(CORES)
        ]
        blocks[step] = lax.ppermute(own, "dp", pairs)
    arrays = []
    for step in range(depth):
        arrays += [blocks[step], lax.ppermute(blocks[step], "dp", swap)]

    rows = 8
    mean, covariance = pl.pallas_call(
        functools.partial(stats_kernel, images, rows, depth),
        grid=(pos_dev // rows,),
        out_shape=[
            jax.ShapeDtypeStruct((pos_dev, CH), jnp.float32),
            jax.ShapeDtypeStruct((CH, pos_dev, CH), jnp.float32),
        ],
        in_specs=[pl.BlockSpec((rows * images, LANES), lambda g: (g, 0))] * dp,
        out_specs=[
            pl.BlockSpec((rows, CH), lambda g: (g, 0)),
            pl.BlockSpec((CH, rows, CH), lambda g: (0, g, 0)),
        ],
        scratch_shapes=[pltpu.VMEM((dp, rows, images, LANES), jnp.float32)],
        compiler_params=pltpu.CompilerParams(vmem_limit_bytes=48 * MIB),
    )(*arrays)
    return mean, jnp.transpose(covariance, (1, 0, 2))


def solution(mesh):
    in_specs = (P(("dp", "pos"), None, None), P(("dp", "pos")), P())
    out_specs = (P("pos", None), P("pos", None, None))
    return jax.shard_map(
        on_device, mesh=mesh, in_specs=in_specs, out_specs=out_specs, check_vma=False
    )
```

```python
import functools

import jax
import jax.numpy as jnp
from jax import lax
from jax.experimental import pallas as pl
from jax.experimental.pallas import tpu as pltpu
from jax.sharding import PartitionSpec as P

CH = 100
CORES = 2
LANES = 128
ROWS = 8
PITCH = ROWS + 1
MIB = 1 << 20


def shift(index, n, step, sign=1):
    if n & (n - 1) == 0:
        return index ^ step
    return (index + sign * step + n) % n


def halves(n):
    small = max(f for f in range(1, n + 1) if n % f == 0 and f * f <= n)
    return small, n // small


def far_first(n_pos, n_z):
    steps = [(p, z) for p in range(n_pos) for z in range(n_z)]
    return sorted(steps, key=sum, reverse=True)[:-1]


def coordinates(dp, pos, dims):
    z_low, pos_low = dims
    z = dp // CORES
    return z // z_low, z % z_low, dp % CORES, pos // pos_low, pos % pos_low


def select_kernel(dims, pos_dev, features_hbm, counts_hbm, order_hbm, *refs):
    pos_low, pos_high = dims
    *out_refs, features_ref, counts_ref, order_ref, picked_ref, sems = refs
    copies = [
        pltpu.make_async_copy(source, target, sems.at[i])
        for i, (source, target) in enumerate(
            ((features_hbm, features_ref), (order_hbm, order_ref), (counts_hbm, counts_ref))
        )
    ]
    for copy in copies:
        copy.start()
    slots, channels, positions = features_ref.shape
    x = lax.axis_index("pos") % pos_low
    lane = lax.broadcasted_iota(jnp.int32, (channels, LANES), 1)
    row = lax.broadcasted_iota(jnp.int32, (channels, LANES), 0)
    flag = lax.broadcasted_iota(jnp.int32, (positions, LANES), 1) == CH
    for copy in reversed(copies):
        copy.wait()
    order = order_ref[...].reshape(1, channels)[:, :LANES]
    picker = jnp.where((row == order) & (lane < CH), 1.0, 0.0).astype(jnp.bfloat16)
    owned = counts_ref[0]
    for slot in range(slots):
        picked = lax.dot_general(
            features_ref[slot], picker, (((0,), (0,)), ((), ())), preferred_element_type=jnp.float32
        )
        picked = jnp.where(flag, 1.0, picked)
        picked_ref[slot] = picked * jnp.where(slot < owned, 1.0, 0.0)
    for step, out_ref in enumerate(out_refs):
        for high in range(pos_high):
            begin = (high * pos_low + shift(x, pos_low, step)) * pos_dev
            begin = pl.multiple_of(begin, pos_dev)
            for slot in range(slots):
                out_ref[pl.ds((high * slots + slot) * pos_dev, pos_dev), :] = picked_ref[
                    slot, pl.ds(begin, pos_dev), :
                ].astype(jnp.bfloat16)


def merge_kernel(dims, slots, pos_dev, *refs):
    z_low, z_high, pos_low, pos_high = dims
    in_refs, out_refs, scratch = refs[: pos_low * z_high], refs[pos_low * z_high : -1], refs[-1]
    z, _, _, y, _ = coordinates(lax.axis_index("dp"), lax.axis_index("pos"), (z_low, pos_low))
    images = len(in_refs) * slots
    size = slots * pos_dev
    for step, out_ref in enumerate(out_refs):
        begin = pl.multiple_of(shift(y, pos_high, step) * size, size)
        for source, ref in enumerate(in_refs):
            pos_step, z_step = source // z_high, source % z_high
            owner = shift(z, z_high, z_step, -1) * pos_low + pos_step
            block = ref[pl.ds(begin, size), :].astype(jnp.float32)
            for slot in range(slots):
                scratch[step, pl.ds(owner * slots + slot, pos_dev, stride=images), :] = block[
                    slot * pos_dev : (slot + 1) * pos_dev
                ]
        out_ref[...] = scratch[step].astype(jnp.bfloat16)


def stats_kernel(dims, images, pos_dev, *refs):
    z_low, z_high, pos_low, pos_high = dims
    blocks = pos_high * z_low * CORES
    in_refs = refs[:blocks]
    mean_hbm, cov_hbm, held, mean_ref, cov_ref, turn_ref, sems = refs[blocks:]
    _, z, core, _, _ = coordinates(lax.axis_index("dp"), lax.axis_index("pos"), (z_low, pos_low))
    for source, ref in enumerate(in_refs):
        pos_step, z_step, core_step = (
            source // (z_low * CORES),
            source // CORES % z_low,
            source % CORES,
        )
        owner = (shift(z, z_low, z_step, -1) * pos_high + pos_step) * CORES + (core ^ core_step)
        held[owner] = ref[...].astype(jnp.float32).reshape(pos_dev, images, LANES)
    everyone = blocks * images
    live = jnp.broadcast_to(
        held[:, 0].reshape(everyone, LANES)[:, CH : CH + 1], (everyone, LANES)
    )
    total = jnp.sum(live, axis=0, keepdims=True)
    factor = 1.0 / (total - 1.0)
    tall = turn_ref.shape[1] // PITCH
    diagonal = lax.broadcasted_iota(jnp.int32, (tall, LANES), 0) == lax.broadcasted_iota(
        jnp.int32, (tall, LANES), 1
    )
    ridge = jnp.where(diagonal, 0.01, 0.0)
    groups = pos_dev // ROWS

    def out(group):
        return pltpu.make_async_copy(
            cov_ref.at[group],
            cov_hbm.at[:, pl.ds(pl.multiple_of(group * ROWS, ROWS), ROWS), :],
            sems.at[group],
        )

    def one_group(group, _):
        for row in range(ROWS):
            position = group * ROWS + row
            samples = held[:, position].reshape(everyone, LANES)
            mean = jnp.sum(samples, axis=0, keepdims=True) / total
            mean_ref[pl.ds(position, 1), :] = mean[:, :CH]
            centered = samples - mean * live
            high = centered.astype(jnp.bfloat16)
            low = (centered - high.astype(jnp.float32)).astype(jnp.bfloat16)
            sums = lax.dot_general(
                jnp.concatenate([high, high, low], axis=0),
                jnp.concatenate([high, low, high], axis=0),
                (((0,), (0,)), ((), ())),
                preferred_element_type=jnp.float32,
            )
            turn_ref[group, pl.ds(row, tall, stride=PITCH), :] = sums[:tall] * factor + ridge
        for channel in range(CH):
            cov_ref[group, channel] = turn_ref[group, pl.ds(channel * PITCH, ROWS), :CH]
        out(group).start()
        return 0

    if everyone > 256:
        lax.fori_loop(0, groups, one_group, 0)
    else:
        for group in range(groups):
            one_group(group, 0)
    mean_out = pltpu.make_async_copy(mean_ref, mean_hbm, sems.at[groups])
    mean_out.start()
    for group in range(groups):
        out(group).wait()
    mean_out.wait()


def on_device(features, counts, channel_order):
    slots, positions, channels = features.shape
    groups, dp = lax.axis_size("pos"), lax.axis_size("dp")
    depth = dp // CORES
    pos_low, pos_high = halves(groups)
    z_low, z_high = halves(depth)
    dims = (z_low, z_high, pos_low, pos_high)
    pos_dev = positions // groups
    images = pos_low * z_high * slots
    wire = jnp.bfloat16
    vmem = pl.BlockSpec(memory_space=pltpu.VMEM)
    hbm = pl.BlockSpec(memory_space=pltpu.HBM)

    def send(block, pos_low_step=0, pos_high_step=0, z_low_step=0, z_high_step=0, core_step=0):
        pairs = []
        for d in range(dp):
            for p in range(groups):
                zh, zl, core, ph, pl_ = coordinates(d, p, (z_low, pos_low))
                z = shift(zh, z_high, z_high_step) * z_low + shift(zl, z_low, z_low_step)
                q = shift(ph, pos_high, pos_high_step) * pos_low + shift(pl_, pos_low, pos_low_step)
                pairs.append((d * groups + p, (z * CORES + (core ^ core_step)) * groups + q))
        return lax.ppermute(block, ("dp", "pos"), pairs)

    half = pos_high * slots * pos_dev
    parts = pl.pallas_call(
        functools.partial(select_kernel, (pos_low, pos_high), pos_dev),
        out_shape=[jax.ShapeDtypeStruct((half, LANES), wire)] * pos_low,
        in_specs=[hbm] * 3,
        out_specs=[vmem] * pos_low,
        scratch_shapes=[
            pltpu.VMEM((slots, channels, positions), wire),
            pltpu.SMEM((1,), jnp.int32),
            pltpu.VMEM((channels,), jnp.int32),
            pltpu.VMEM((slots, positions, LANES), jnp.float32),
            pltpu.SemaphoreType.DMA((3,)),
        ],
        compiler_params=pltpu.CompilerParams(vmem_limit_bytes=16 * MIB),
    )(
        pltpu.with_memory_space_constraint(jnp.transpose(features, (0, 2, 1)), pltpu.HBM),
        counts,
        pltpu.with_memory_space_constraint(channel_order, pltpu.HBM),
    )

    got = {(0, 0): parts[0]}
    for step in far_first(pos_low, z_high):
        got[step] = send(parts[step[0]], pos_low_step=step[0], z_high_step=step[1])

    owns = pl.pallas_call(
        functools.partial(merge_kernel, dims, slots, pos_dev),
        out_shape=[jax.ShapeDtypeStruct((pos_dev * images, LANES), wire)] * pos_high,
        in_specs=[vmem] * (pos_low * z_high),
        out_specs=[vmem] * pos_high,
        scratch_shapes=[pltpu.VMEM((pos_high, pos_dev * images, LANES), jnp.float32)],
        compiler_params=pltpu.CompilerParams(vmem_limit_bytes=32 * MIB),
    )(*(got[p, z] for p in range(pos_low) for z in range(z_high)))

    near = {(0, 0): owns[0]}
    for step in far_first(pos_high, z_low):
        near[step] = send(owns[step[0]], pos_high_step=step[0], z_low_step=step[1])
    arrays = []
    for p in range(pos_high):
        for z in range(z_low):
            arrays += [near[p, z], send(near[p, z], core_step=1)]

    tall = -(-CH // ROWS) * ROWS
    mean, covariance = pl.pallas_call(
        functools.partial(stats_kernel, dims, images, pos_dev),
        out_shape=[
            jax.ShapeDtypeStruct((pos_dev, CH), jnp.float32),
            jax.ShapeDtypeStruct((CH, pos_dev, CH), jnp.float32),
        ],
        in_specs=[vmem] * len(arrays),
        out_specs=[hbm, hbm],
        scratch_shapes=[
            pltpu.VMEM((len(arrays), pos_dev, images, LANES), jnp.float32),
            pltpu.VMEM((pos_dev, CH), jnp.float32),
            pltpu.VMEM((pos_dev // ROWS, CH, ROWS, CH), jnp.float32),
            pltpu.VMEM((pos_dev // ROWS, tall * PITCH, LANES), jnp.float32),
            pltpu.SemaphoreType.DMA((pos_dev // ROWS + 1,)),
        ],
        compiler_params=pltpu.CompilerParams(vmem_limit_bytes=48 * MIB),
    )(*arrays)
    return mean, jnp.transpose(covariance, (1, 0, 2))


def solution(mesh):
    in_specs = (P(("dp", "pos"), None, None), P(("dp", "pos")), P())
    out_specs = (P("pos", None), P("pos", None, None))
    return jax.shard_map(
        on_device, mesh=mesh, in_specs=in_specs, out_specs=out_specs, check_vma=False
    )
```

```python
import functools

import jax
import jax.numpy as jnp
from jax import lax
from jax.experimental import pallas as pl
from jax.experimental.pallas import tpu as pltpu
from jax.sharding import PartitionSpec as P

CH = 100
CORES = 2
LANES = 128
ROWS = 8
PITCH = ROWS + 1
MIB = 1 << 20


def shift(index, n, step, sign=1):
    if n & (n - 1) == 0:
        return index ^ step
    return (index + sign * step + n) % n


def halves(n):
    small = max(f for f in range(1, n + 1) if n % f == 0 and f * f <= n)
    return small, n // small


def far_first(n_pos, n_z):
    steps = [(p, z) for p in range(n_pos) for z in range(n_z)]
    return sorted(steps, key=sum, reverse=True)[:-1]


def coordinates(dp, pos, dims):
    z_low, pos_low = dims
    z = dp // CORES
    return z // z_low, z % z_low, dp % CORES, pos // pos_low, pos % pos_low


def select_kernel(dims, pos_dev, features_hbm, counts_hbm, order_hbm, *refs):
    pos_low, pos_high = dims
    *out_refs, features_ref, counts_ref, order_ref, picked_ref, sems = refs
    copies = [
        pltpu.make_async_copy(source, target, sems.at[i])
        for i, (source, target) in enumerate(
            ((features_hbm, features_ref), (order_hbm, order_ref), (counts_hbm, counts_ref))
        )
    ]
    for copy in copies:
        copy.start()
    slots, channels, positions = features_ref.shape
    x = lax.axis_index("pos") % pos_low
    lane = lax.broadcasted_iota(jnp.int32, (channels, LANES), 1)
    row = lax.broadcasted_iota(jnp.int32, (channels, LANES), 0)
    flag = lax.broadcasted_iota(jnp.int32, (positions, LANES), 1) == CH
    for copy in reversed(copies):
        copy.wait()
    order = order_ref[...].reshape(1, channels)[:, :LANES]
    picker = jnp.where((row == order) & (lane < CH), 1.0, 0.0).astype(jnp.bfloat16)
    owned = counts_ref[0]
    for slot in range(slots):
        picked = lax.dot_general(
            features_ref[slot], picker, (((0,), (0,)), ((), ())), preferred_element_type=jnp.float32
        )
        picked = jnp.where(flag, 1.0, picked)
        picked_ref[slot] = picked * jnp.where(slot < owned, 1.0, 0.0)
    for step, out_ref in enumerate(out_refs):
        for high in range(pos_high):
            begin = (high * pos_low + shift(x, pos_low, step)) * pos_dev
            begin = pl.multiple_of(begin, pos_dev)
            for slot in range(slots):
                out_ref[pl.ds((high * slots + slot) * pos_dev, pos_dev), :] = picked_ref[
                    slot, pl.ds(begin, pos_dev), :
                ].astype(jnp.bfloat16)


def merge_kernel(dims, slots, pos_dev, *refs):
    z_low, z_high, pos_low, pos_high = dims
    in_refs, out_refs, scratch = refs[: pos_low * z_high], refs[pos_low * z_high : -1], refs[-1]
    z, _, _, y, _ = coordinates(lax.axis_index("dp"), lax.axis_index("pos"), (z_low, pos_low))
    images = len(in_refs) * slots
    size = slots * pos_dev
    for step, out_ref in enumerate(out_refs):
        begin = pl.multiple_of(shift(y, pos_high, step) * size, size)
        for source, ref in enumerate(in_refs):
            pos_step, z_step = source // z_high, source % z_high
            owner = shift(z, z_high, z_step, -1) * pos_low + pos_step
            block = ref[pl.ds(begin, size), :].astype(jnp.float32)
            for slot in range(slots):
                scratch[step, pl.ds(owner * slots + slot, pos_dev, stride=images), :] = block[
                    slot * pos_dev : (slot + 1) * pos_dev
                ]
        out_ref[...] = scratch[step].astype(jnp.bfloat16)


def stats_kernel(dims, images, pos_dev, *refs):
    z_low, z_high, pos_low, pos_high = dims
    blocks = pos_high * z_low * CORES
    in_refs = refs[:blocks]
    mean_hbm, cov_hbm, held, mean_ref, cov_ref, turn_ref, sems = refs[blocks:]
    z_top, z, core, _, _ = coordinates(lax.axis_index("dp"), lax.axis_index("pos"), (z_low, pos_low))
    slot = lax.broadcasted_iota(jnp.int32, (1, images, LANES), 1)
    kept = slot // (images // (z_high * pos_low)) == z_top * pos_low
    for pair in range(blocks // CORES):
        pos_step, z_step = pair // z_low, pair % z_low
        base = (shift(z, z_low, z_step, -1) * pos_high + pos_step) * CORES
        near = core if pair == 0 else 1 - core
        first, second = (
            in_refs[pair * CORES + i][...].astype(jnp.float32).reshape(pos_dev, images, LANES)
            for i in range(CORES)
        )
        held[base + near] = jnp.where(kept, first, second)
        held[base + 1 - near] = jnp.where(kept, second, first)
    everyone = blocks * images
    live = jnp.broadcast_to(
        held[:, 0].reshape(everyone, LANES)[:, CH : CH + 1], (everyone, LANES)
    )
    total = jnp.sum(live, axis=0, keepdims=True)
    factor = 1.0 / (total - 1.0)
    tall = turn_ref.shape[1] // PITCH
    diagonal = lax.broadcasted_iota(jnp.int32, (tall, LANES), 0) == lax.broadcasted_iota(
        jnp.int32, (tall, LANES), 1
    )
    ridge = jnp.where(diagonal, 0.01, 0.0)
    groups = pos_dev // ROWS

    def out(group):
        return pltpu.make_async_copy(
            cov_ref.at[group],
            cov_hbm.at[:, pl.ds(pl.multiple_of(group * ROWS, ROWS), ROWS), :],
            sems.at[group],
        )

    def one_group(group, _):
        for row in range(ROWS):
            position = group * ROWS + row
            samples = held[:, position].reshape(everyone, LANES)
            mean = jnp.sum(samples, axis=0, keepdims=True) / total
            mean_ref[pl.ds(position, 1), :] = mean[:, :CH]
            centered = samples - mean * live
            high = centered.astype(jnp.bfloat16)
            low = (centered - high.astype(jnp.float32)).astype(jnp.bfloat16)
            sums = lax.dot_general(
                jnp.concatenate([high, high, low], axis=0),
                jnp.concatenate([high, low, high], axis=0),
                (((0,), (0,)), ((), ())),
                preferred_element_type=jnp.float32,
            )
            turn_ref[group, pl.ds(row, tall, stride=PITCH), :] = sums[:tall] * factor + ridge
        for channel in range(CH):
            cov_ref[group, channel] = turn_ref[group, pl.ds(channel * PITCH, ROWS), :CH]
        out(group).start()
        return 0

    if everyone > 256:
        lax.fori_loop(0, groups, one_group, 0)
    else:
        for group in range(groups):
            one_group(group, 0)
    mean_out = pltpu.make_async_copy(mean_ref, mean_hbm, sems.at[groups])
    mean_out.start()
    for group in range(groups):
        out(group).wait()
    mean_out.wait()


def on_device(features, counts, channel_order):
    slots, positions, channels = features.shape
    groups, dp = lax.axis_size("pos"), lax.axis_size("dp")
    depth = dp // CORES
    pos_low, pos_high = halves(groups)
    z_low, z_high = halves(depth)
    dims = (z_low, z_high, pos_low, pos_high)
    pos_dev = positions // groups
    images = pos_low * z_high * slots
    wire = jnp.bfloat16
    vmem = pl.BlockSpec(memory_space=pltpu.VMEM)
    hbm = pl.BlockSpec(memory_space=pltpu.HBM)

    def send(block, pos_low_step=0, pos_high_step=0, z_low_step=0, z_high_step=0, core_step=0):
        pairs = []
        for d in range(dp):
            for p in range(groups):
                zh, zl, core, ph, pl_ = coordinates(d, p, (z_low, pos_low))
                z = shift(zh, z_high, z_high_step) * z_low + shift(zl, z_low, z_low_step)
                q = shift(ph, pos_high, pos_high_step) * pos_low + shift(pl_, pos_low, pos_low_step)
                pairs.append((d * groups + p, (z * CORES + (core ^ core_step)) * groups + q))
        return lax.ppermute(block, ("dp", "pos"), pairs)

    half = pos_high * slots * pos_dev
    parts = pl.pallas_call(
        functools.partial(select_kernel, (pos_low, pos_high), pos_dev),
        out_shape=[jax.ShapeDtypeStruct((half, LANES), wire)] * pos_low,
        in_specs=[hbm] * 3,
        out_specs=[vmem] * pos_low,
        scratch_shapes=[
            pltpu.VMEM((slots, channels, positions), wire),
            pltpu.SMEM((1,), jnp.int32),
            pltpu.VMEM((channels,), jnp.int32),
            pltpu.VMEM((slots, positions, LANES), jnp.float32),
            pltpu.SemaphoreType.DMA((3,)),
        ],
        compiler_params=pltpu.CompilerParams(vmem_limit_bytes=16 * MIB),
    )(
        pltpu.with_memory_space_constraint(jnp.transpose(features, (0, 2, 1)), pltpu.HBM),
        counts,
        pltpu.with_memory_space_constraint(channel_order, pltpu.HBM),
    )

    got = {(0, 0): parts[0]}
    for step in far_first(pos_low, z_high):
        got[step] = send(parts[step[0]], pos_low_step=step[0], z_high_step=step[1], core_step=1)

    owns = pl.pallas_call(
        functools.partial(merge_kernel, dims, slots, pos_dev),
        out_shape=[jax.ShapeDtypeStruct((pos_dev * images, LANES), wire)] * pos_high,
        in_specs=[vmem] * (pos_low * z_high),
        out_specs=[vmem] * pos_high,
        scratch_shapes=[pltpu.VMEM((pos_high, pos_dev * images, LANES), jnp.float32)],
        compiler_params=pltpu.CompilerParams(vmem_limit_bytes=32 * MIB),
    )(*(got[p, z] for p in range(pos_low) for z in range(z_high)))

    near = {(0, 0): owns[0]}
    for step in far_first(pos_high, z_low):
        near[step] = send(owns[step[0]], pos_high_step=step[0], z_low_step=step[1], core_step=1)
    arrays = []
    for p in range(pos_high):
        for z in range(z_low):
            arrays += [near[p, z], send(near[p, z], core_step=1)]

    tall = -(-CH // ROWS) * ROWS
    mean, covariance = pl.pallas_call(
        functools.partial(stats_kernel, dims, images, pos_dev),
        out_shape=[
            jax.ShapeDtypeStruct((pos_dev, CH), jnp.float32),
            jax.ShapeDtypeStruct((CH, pos_dev, CH), jnp.float32),
        ],
        in_specs=[vmem] * len(arrays),
        out_specs=[hbm, hbm],
        scratch_shapes=[
            pltpu.VMEM((len(arrays), pos_dev, images, LANES), jnp.float32),
            pltpu.VMEM((pos_dev, CH), jnp.float32),
            pltpu.VMEM((pos_dev // ROWS, CH, ROWS, CH), jnp.float32),
            pltpu.VMEM((pos_dev // ROWS, tall * PITCH, LANES), jnp.float32),
            pltpu.SemaphoreType.DMA((pos_dev // ROWS + 1,)),
        ],
        compiler_params=pltpu.CompilerParams(vmem_limit_bytes=48 * MIB),
    )(*arrays)
    return mean, jnp.transpose(covariance, (1, 0, 2))


def solution(mesh):
    in_specs = (P(("dp", "pos"), None, None), P(("dp", "pos")), P())
    out_specs = (P("pos", None), P("pos", None, None))
    return jax.shard_map(
        on_device, mesh=mesh, in_specs=in_specs, out_specs=out_specs, check_vma=False
    )
```

```python
import functools

import jax
import jax.numpy as jnp
from jax import lax
from jax.experimental import pallas as pl
from jax.experimental.pallas import tpu as pltpu
from jax.sharding import PartitionSpec as P

CH = 100
CORES = 2
LANES = 128
ROWS = 8
PITCH = ROWS + 1
MIB = 1 << 20


def shift(index, n, step, sign=1):
    if n & (n - 1) == 0:
        return index ^ step
    return (index + sign * step + n) % n


def halves(n):
    small = max(f for f in range(1, n + 1) if n % f == 0 and f * f <= n)
    return small, n // small


def far_first(n_pos, n_z):
    steps = [(p, z) for p in range(n_pos) for z in range(n_z)]
    return sorted(steps, key=sum, reverse=True)[:-1]


def coordinates(dp, pos, dims):
    z_low, pos_low = dims
    z = dp // CORES
    return z // z_low, z % z_low, dp % CORES, pos // pos_low, pos % pos_low


def select_kernel(dims, pos_dev, features_hbm, counts_ref, order_hbm, *refs):
    pos_low, pos_high = dims
    *out_refs, features_ref, order_ref, picked_ref, sems = refs
    order_copy = pltpu.make_async_copy(order_hbm, order_ref, sems.at[0])
    feature_copies = [pltpu.make_async_copy(features_hbm, features_ref, sems.at[1])]
    for copy in feature_copies:
        copy.start()
    order_copy.start()
    slots, channels, positions = features_ref.shape
    x = lax.axis_index("pos") % pos_low
    lane = lax.broadcasted_iota(jnp.int32, (channels, LANES), 1)
    row = lax.broadcasted_iota(jnp.int32, (channels, LANES), 0)
    flag = lax.broadcasted_iota(jnp.int32, (positions, LANES), 1) == CH
    owned = counts_ref[0]
    order_copy.wait()
    order = order_ref[...].reshape(1, channels)[:, :LANES]
    picker = jnp.where((row == order) & (lane < CH), 1.0, 0.0).astype(jnp.bfloat16)
    for copy in feature_copies:
        copy.wait()
    for slot in range(slots):
        picked = lax.dot_general(
            features_ref[slot], picker, (((0,), (0,)), ((), ())), preferred_element_type=jnp.float32
        )
        picked = jnp.where(flag, 1.0, picked)
        picked_ref[slot] = picked * jnp.where(slot < owned, 1.0, 0.0)
    for step, out_ref in enumerate(out_refs):
        for high in range(pos_high):
            begin = (high * pos_low + shift(x, pos_low, step)) * pos_dev
            begin = pl.multiple_of(begin, pos_dev)
            for slot in range(slots):
                out_ref[pl.ds((high * slots + slot) * pos_dev, pos_dev), :] = picked_ref[
                    slot, pl.ds(begin, pos_dev), :
                ].astype(jnp.bfloat16)


def merge_kernel(dims, slots, pos_dev, *refs):
    z_low, z_high, pos_low, pos_high = dims
    in_refs, out_refs, scratch = refs[: pos_low * z_high], refs[pos_low * z_high : -1], refs[-1]
    z, _, _, y, _ = coordinates(lax.axis_index("dp"), lax.axis_index("pos"), (z_low, pos_low))
    images = len(in_refs) * slots
    size = slots * pos_dev
    for step, out_ref in enumerate(out_refs):
        begin = pl.multiple_of(shift(y, pos_high, step) * size, size)
        for source, ref in enumerate(in_refs):
            pos_step, z_step = source // z_high, source % z_high
            owner = shift(z, z_high, z_step, -1) * pos_low + pos_step
            block = ref[pl.ds(begin, size), :].astype(jnp.float32)
            for slot in range(slots):
                scratch[step, pl.ds(owner * slots + slot, pos_dev, stride=images), :] = block[
                    slot * pos_dev : (slot + 1) * pos_dev
                ]
        out_ref[...] = scratch[step].astype(jnp.bfloat16)


def stats_kernel(dims, images, pos_dev, *refs):
    z_low, z_high, pos_low, pos_high = dims
    blocks = pos_high * z_low * CORES
    in_refs = refs[:blocks]
    mean_hbm, cov_hbm, held, mean_ref, cov_ref, turn_ref, sems = refs[blocks:]
    z_top, z, core, _, _ = coordinates(lax.axis_index("dp"), lax.axis_index("pos"), (z_low, pos_low))
    slot = lax.broadcasted_iota(jnp.int32, (1, images, LANES), 1)
    kept = slot // (images // (z_high * pos_low)) == z_top * pos_low
    for pair in range(blocks // CORES):
        pos_step, z_step = pair // z_low, pair % z_low
        base = (shift(z, z_low, z_step, -1) * pos_high + pos_step) * CORES
        near = core if pair == 0 else 1 - core
        first, second = (
            in_refs[pair * CORES + i][...].astype(jnp.float32).reshape(pos_dev, images, LANES)
            for i in range(CORES)
        )
        held[base + near] = jnp.where(kept, first, second)
        held[base + 1 - near] = jnp.where(kept, second, first)
    everyone = blocks * images
    live = jnp.broadcast_to(
        held[:, 0].reshape(everyone, LANES)[:, CH : CH + 1], (everyone, LANES)
    )
    total = jnp.sum(live, axis=0, keepdims=True)
    factor = 1.0 / (total - 1.0)
    tall = turn_ref.shape[1] // PITCH
    diagonal = lax.broadcasted_iota(jnp.int32, (tall, LANES), 0) == lax.broadcasted_iota(
        jnp.int32, (tall, LANES), 1
    )
    ridge = jnp.where(diagonal, 0.01, 0.0)
    groups = pos_dev // ROWS

    def out(group):
        return pltpu.make_async_copy(
            cov_ref.at[group],
            cov_hbm.at[:, pl.ds(pl.multiple_of(group * ROWS, ROWS), ROWS), :],
            sems.at[group],
        )

    def one_group(group, _):
        for row in range(ROWS):
            position = group * ROWS + row
            samples = held[:, position].reshape(everyone, LANES)
            mean = jnp.sum(samples, axis=0, keepdims=True) / total
            mean_ref[pl.ds(position, 1), :] = mean[:, :CH]
            centered = samples - mean * live
            high = centered.astype(jnp.bfloat16)
            low = (centered - high.astype(jnp.float32)).astype(jnp.bfloat16)
            both = jnp.swapaxes(jnp.concatenate([high, low], axis=0), 0, 1)[:tall]
            sums = lax.dot_general(
                jnp.concatenate([both, both], axis=1),
                jnp.concatenate([high, high, low, jnp.zeros_like(low)], axis=0),
                (((1,), (0,)), ((), ())),
                preferred_element_type=jnp.float32,
            )
            turn_ref[group, pl.ds(row, tall, stride=PITCH), :] = sums * factor + ridge
        for channel in range(CH):
            cov_ref[group, channel] = turn_ref[group, pl.ds(channel * PITCH, ROWS), :CH]
        out(group).start()
        return 0

    if everyone > 256:
        lax.fori_loop(0, groups, one_group, 0)
    else:
        for group in range(groups):
            one_group(group, 0)
    mean_out = pltpu.make_async_copy(mean_ref, mean_hbm, sems.at[groups])
    mean_out.start()
    for group in range(groups):
        out(group).wait()
    mean_out.wait()


def on_device(features, counts, channel_order):
    slots, positions, channels = features.shape
    groups, dp = lax.axis_size("pos"), lax.axis_size("dp")
    depth = dp // CORES
    pos_low, pos_high = halves(groups)
    z_low, z_high = halves(depth)
    dims = (z_low, z_high, pos_low, pos_high)
    pos_dev = positions // groups
    images = pos_low * z_high * slots
    wire = jnp.bfloat16
    vmem = pl.BlockSpec(memory_space=pltpu.VMEM)
    hbm = pl.BlockSpec(memory_space=pltpu.HBM)

    def send(block, pos_low_step=0, pos_high_step=0, z_low_step=0, z_high_step=0, core_step=0):
        pairs = []
        for d in range(dp):
            for p in range(groups):
                zh, zl, core, ph, pl_ = coordinates(d, p, (z_low, pos_low))
                z = shift(zh, z_high, z_high_step) * z_low + shift(zl, z_low, z_low_step)
                q = shift(ph, pos_high, pos_high_step) * pos_low + shift(pl_, pos_low, pos_low_step)
                pairs.append((d * groups + p, (z * CORES + (core ^ core_step)) * groups + q))
        return lax.ppermute(block, ("dp", "pos"), pairs)

    half = pos_high * slots * pos_dev
    parts = pl.pallas_call(
        functools.partial(select_kernel, (pos_low, pos_high), pos_dev),
        out_shape=[jax.ShapeDtypeStruct((half, LANES), wire)] * pos_low,
        in_specs=[hbm, pl.BlockSpec(memory_space=pltpu.SMEM), hbm],
        out_specs=[vmem] * pos_low,
        scratch_shapes=[
            pltpu.VMEM((slots, channels, positions), wire),
            pltpu.VMEM((channels,), jnp.int32),
            pltpu.VMEM((slots, positions, LANES), jnp.float32),
            pltpu.SemaphoreType.DMA((1 + slots,)),
        ],
        compiler_params=pltpu.CompilerParams(vmem_limit_bytes=16 * MIB),
    )(
        pltpu.with_memory_space_constraint(jnp.transpose(features, (0, 2, 1)), pltpu.HBM),
        counts,
        pltpu.with_memory_space_constraint(channel_order, pltpu.HBM),
    )

    got = {(0, 0): parts[0]}
    for step in far_first(pos_low, z_high):
        got[step] = send(parts[step[0]], pos_low_step=step[0], z_high_step=step[1], core_step=1)

    owns = pl.pallas_call(
        functools.partial(merge_kernel, dims, slots, pos_dev),
        out_shape=[jax.ShapeDtypeStruct((pos_dev * images, LANES), wire)] * pos_high,
        in_specs=[vmem] * (pos_low * z_high),
        out_specs=[vmem] * pos_high,
        scratch_shapes=[pltpu.VMEM((pos_high, pos_dev * images, LANES), jnp.float32)],
        compiler_params=pltpu.CompilerParams(vmem_limit_bytes=32 * MIB),
    )(*(got[p, z] for p in range(pos_low) for z in range(z_high)))

    near = {(0, 0): owns[0]}
    for step in far_first(pos_high, z_low):
        near[step] = send(owns[step[0]], pos_high_step=step[0], z_low_step=step[1], core_step=1)
    arrays = []
    for p in range(pos_high):
        for z in range(z_low):
            arrays += [near[p, z], send(near[p, z], core_step=1)]

    tall = -(-CH // ROWS) * ROWS
    mean, covariance = pl.pallas_call(
        functools.partial(stats_kernel, dims, images, pos_dev),
        out_shape=[
            jax.ShapeDtypeStruct((pos_dev, CH), jnp.float32),
            jax.ShapeDtypeStruct((CH, pos_dev, CH), jnp.float32),
        ],
        in_specs=[vmem] * len(arrays),
        out_specs=[hbm, hbm],
        scratch_shapes=[
            pltpu.VMEM((len(arrays), pos_dev, images, LANES), jnp.float32),
            pltpu.VMEM((pos_dev, CH), jnp.float32),
            pltpu.VMEM((pos_dev // ROWS, CH, ROWS, CH), jnp.float32),
            pltpu.VMEM((pos_dev // ROWS, tall * PITCH, LANES), jnp.float32),
            pltpu.SemaphoreType.DMA((pos_dev // ROWS + 1,)),
        ],
        compiler_params=pltpu.CompilerParams(vmem_limit_bytes=48 * MIB),
    )(*arrays)
    return mean, jnp.transpose(covariance, (1, 0, 2))


def solution(mesh):
    in_specs = (P(("dp", "pos"), None, None), P(("dp", "pos")), P())
    out_specs = (P("pos", None), P("pos", None, None))
    return jax.shard_map(
        on_device, mesh=mesh, in_specs=in_specs, out_specs=out_specs, check_vma=False
    )
```

```python
import functools

import jax
import jax.numpy as jnp
from jax import lax
from jax.experimental import pallas as pl
from jax.experimental.pallas import tpu as pltpu
from jax.sharding import PartitionSpec as P

CH = 100
CORES = 2
LANES = 128
ROWS = 8
PITCH = ROWS + 1
MIB = 1 << 20
PIECES = 4
PIECE = CH // PIECES


def packing(pos_dev):
    extra = (pos_dev - 1) // (PIECES + 1)
    return pos_dev - extra, extra


def unpack(ref, images, pos_dev):
    block = ref[...].astype(jnp.float32)
    size = packing(pos_dev)[1] * images
    place = lax.broadcasted_iota(jnp.int32, (size, LANES), 1) // PIECE
    moved = None
    for piece in range(PIECES):
        part = pltpu.roll(block[piece * size : (piece + 1) * size], LANES - CH + piece * PIECE, 1)
        moved = part if moved is None else jnp.where(place == piece, part, moved)
    return jnp.concatenate([block, moved], axis=0).reshape(pos_dev, images, LANES)


def shift(index, n, step, sign=1):
    if n & (n - 1) == 0:
        return index ^ step
    return (index + sign * step + n) % n


def halves(n):
    small = max(f for f in range(1, n + 1) if n % f == 0 and f * f <= n)
    return small, n // small


def far_first(n_pos, n_z):
    steps = [(p, z) for p in range(n_pos) for z in range(n_z)]
    return sorted(steps, key=sum, reverse=True)[:-1]


def coordinates(dp, pos, dims):
    z_low, pos_low = dims
    z = dp // CORES
    return z // z_low, z % z_low, dp % CORES, pos // pos_low, pos % pos_low


def select_kernel(dims, pos_dev, features_hbm, counts_ref, order_hbm, *refs):
    pos_low, pos_high = dims
    *out_refs, features_ref, order_ref, picked_ref, sems = refs
    order_copy = pltpu.make_async_copy(order_hbm, order_ref, sems.at[0])
    feature_copies = [pltpu.make_async_copy(features_hbm, features_ref, sems.at[1])]
    for copy in feature_copies:
        copy.start()
    order_copy.start()
    slots, channels, positions = features_ref.shape
    x = lax.axis_index("pos") % pos_low
    lane = lax.broadcasted_iota(jnp.int32, (channels, LANES), 1)
    row = lax.broadcasted_iota(jnp.int32, (channels, LANES), 0)
    flag = lax.broadcasted_iota(jnp.int32, (positions, LANES), 1) == CH
    owned = counts_ref[0]
    order_copy.wait()
    order = order_ref[...].reshape(1, channels)[:, :LANES]
    picker = jnp.where((row == order) & (lane < CH), 1.0, 0.0).astype(jnp.bfloat16)
    for copy in feature_copies:
        copy.wait()
    for slot in range(slots):
        picked = lax.dot_general(
            features_ref[slot], picker, (((0,), (0,)), ((), ())), preferred_element_type=jnp.float32
        )
        picked = jnp.where(flag, 1.0, picked)
        picked_ref[slot] = picked * jnp.where(slot < owned, 1.0, 0.0)
    for step, out_ref in enumerate(out_refs):
        for high in range(pos_high):
            begin = (high * pos_low + shift(x, pos_low, step)) * pos_dev
            begin = pl.multiple_of(begin, pos_dev)
            for slot in range(slots):
                out_ref[pl.ds((high * slots + slot) * pos_dev, pos_dev), :] = picked_ref[
                    slot, pl.ds(begin, pos_dev), :
                ].astype(jnp.bfloat16)


def merge_kernel(dims, slots, pos_dev, *refs):
    z_low, z_high, pos_low, pos_high = dims
    in_refs, out_refs, scratch = refs[: pos_low * z_high], refs[pos_low * z_high : -1], refs[-1]
    z, _, _, y, _ = coordinates(lax.axis_index("dp"), lax.axis_index("pos"), (z_low, pos_low))
    images = len(in_refs) * slots
    size = slots * pos_dev
    for step, out_ref in enumerate(out_refs):
        begin = pl.multiple_of(shift(y, pos_high, step) * size, size)
        for source, ref in enumerate(in_refs):
            pos_step, z_step = source // z_high, source % z_high
            owner = shift(z, z_high, z_step, -1) * pos_low + pos_step
            block = ref[pl.ds(begin, size), :].astype(jnp.float32)
            for slot in range(slots):
                scratch[step, pl.ds(owner * slots + slot, pos_dev, stride=images), :] = block[
                    slot * pos_dev : (slot + 1) * pos_dev
                ]
        base, extra = packing(pos_dev)
        size_extra = extra * images
        own = lax.broadcasted_iota(jnp.int32, (size_extra, LANES), 1) < CH
        moved = scratch[step, pl.ds(base * images, size_extra), :]
        for piece in range(PIECES):
            rows = pl.ds(piece * size_extra, size_extra)
            turned = pltpu.roll(moved, CH - piece * PIECE, 1)
            out_ref[rows, :] = jnp.where(own, scratch[step, rows, :], turned).astype(jnp.bfloat16)
        rows = pl.ds(PIECES * size_extra, base * images - PIECES * size_extra)
        out_ref[rows, :] = scratch[step, rows, :].astype(jnp.bfloat16)


def places(dims, images):
    z_low, z_high, pos_low, pos_high = dims
    z_top, z, core, _, _ = coordinates(lax.axis_index("dp"), lax.axis_index("pos"), (z_low, pos_low))
    slot = lax.broadcasted_iota(jnp.int32, (1, images, LANES), 1)
    kept = slot // (images // (z_high * pos_low)) == z_top * pos_low
    where = {}
    for p in range(pos_high):
        for step in range(z_low):
            index = (shift(z, z_low, step, -1) * pos_high + p) * CORES
            near = core if p + step == 0 else 1 - core
            where[p, step] = (index + near, index + 1 - near)
    return kept, where


def put(held, kept, where, first, second):
    held[where[0]] = jnp.where(kept, first, second)
    held[where[1]] = jnp.where(kept, second, first)


def prepare_kernel(dims, images, pos_dev, whole, half, *refs):
    *in_refs, held = refs
    kept, where = places(dims, images)
    for i, step in enumerate(whole):
        first, second = (unpack(in_refs[CORES * i + j], images, pos_dev) for j in range(CORES))
        put(held, kept, where[step], first, second)
    for i, step in enumerate(half):
        held[where[step][0]] = unpack(in_refs[CORES * len(whole) + i], images, pos_dev)


def stats_kernel(dims, images, pos_dev, half, *refs):
    z_low, z_high, pos_low, pos_high = dims
    blocks = pos_high * z_low * CORES
    _, *in_refs = refs[: 1 + len(half)]
    mean_hbm, cov_hbm, held, mean_ref, cov_ref, turn_ref, sems = refs[1 + len(half) :]
    kept, where = places(dims, images)
    for step, ref in zip(half, in_refs):
        put(held, kept, where[step], held[where[step][0]], unpack(ref, images, pos_dev))
    base = packing(pos_dev)[0]
    everyone = blocks * images
    live = jnp.broadcast_to(
        held[:, base - 1].reshape(everyone, LANES)[:, CH : CH + 1], (everyone, LANES)
    )
    total = jnp.sum(live, axis=0, keepdims=True)
    factor = 1.0 / (total - 1.0)
    tall = turn_ref.shape[1] // PITCH
    diagonal = lax.broadcasted_iota(jnp.int32, (tall, LANES), 0) == lax.broadcasted_iota(
        jnp.int32, (tall, LANES), 1
    )
    ridge = jnp.where(diagonal, 0.01, 0.0)
    groups = pos_dev // ROWS

    def out(group):
        return pltpu.make_async_copy(
            cov_ref.at[group],
            cov_hbm.at[:, pl.ds(pl.multiple_of(group * ROWS, ROWS), ROWS), :],
            sems.at[group],
        )

    def one_group(group, _):
        for row in range(ROWS):
            position = group * ROWS + row
            samples = held[:, position].reshape(everyone, LANES)
            mean = jnp.sum(samples, axis=0, keepdims=True) / total
            mean_ref[pl.ds(position, 1), :] = mean[:, :CH]
            centered = samples - mean * live
            high = centered.astype(jnp.bfloat16)
            low = (centered - high.astype(jnp.float32)).astype(jnp.bfloat16)
            both = jnp.swapaxes(jnp.concatenate([high, low], axis=0), 0, 1)[:tall]
            sums = lax.dot_general(
                jnp.concatenate([both, both], axis=1),
                jnp.concatenate([high, high, low, jnp.zeros_like(low)], axis=0),
                (((1,), (0,)), ((), ())),
                preferred_element_type=jnp.float32,
            )
            turn_ref[group, pl.ds(row, tall, stride=PITCH), :] = sums * factor + ridge
        for channel in range(CH):
            cov_ref[group, channel] = turn_ref[group, pl.ds(channel * PITCH, ROWS), :CH]
        out(group).start()
        return 0

    if everyone > 256:
        lax.fori_loop(0, groups, one_group, 0)
    else:
        for group in range(groups):
            one_group(group, 0)
    mean_out = pltpu.make_async_copy(mean_ref, mean_hbm, sems.at[groups])
    mean_out.start()
    for group in range(groups):
        out(group).wait()
    mean_out.wait()


def on_device(features, counts, channel_order):
    slots, positions, channels = features.shape
    groups, dp = lax.axis_size("pos"), lax.axis_size("dp")
    depth = dp // CORES
    pos_low, pos_high = halves(groups)
    z_low, z_high = halves(depth)
    dims = (z_low, z_high, pos_low, pos_high)
    pos_dev = positions // groups
    images = pos_low * z_high * slots
    wire = jnp.bfloat16
    vmem = pl.BlockSpec(memory_space=pltpu.VMEM)
    hbm = pl.BlockSpec(memory_space=pltpu.HBM)

    def send(block, pos_low_step=0, pos_high_step=0, z_low_step=0, z_high_step=0, core_step=0):
        pairs = []
        for d in range(dp):
            for p in range(groups):
                zh, zl, core, ph, pl_ = coordinates(d, p, (z_low, pos_low))
                z = shift(zh, z_high, z_high_step) * z_low + shift(zl, z_low, z_low_step)
                q = shift(ph, pos_high, pos_high_step) * pos_low + shift(pl_, pos_low, pos_low_step)
                pairs.append((d * groups + p, (z * CORES + (core ^ core_step)) * groups + q))
        return lax.ppermute(block, ("dp", "pos"), pairs)

    half = pos_high * slots * pos_dev
    parts = pl.pallas_call(
        functools.partial(select_kernel, (pos_low, pos_high), pos_dev),
        out_shape=[jax.ShapeDtypeStruct((half, LANES), wire)] * pos_low,
        in_specs=[hbm, pl.BlockSpec(memory_space=pltpu.SMEM), hbm],
        out_specs=[vmem] * pos_low,
        scratch_shapes=[
            pltpu.VMEM((slots, channels, positions), wire),
            pltpu.VMEM((channels,), jnp.int32),
            pltpu.VMEM((slots, positions, LANES), jnp.float32),
            pltpu.SemaphoreType.DMA((1 + slots,)),
        ],
        compiler_params=pltpu.CompilerParams(vmem_limit_bytes=16 * MIB),
    )(
        pltpu.with_memory_space_constraint(jnp.transpose(features, (0, 2, 1)), pltpu.HBM),
        counts,
        pltpu.with_memory_space_constraint(channel_order, pltpu.HBM),
    )

    got = {(0, 0): parts[0]}
    for step in far_first(pos_low, z_high):
        got[step] = send(parts[step[0]], pos_low_step=step[0], z_high_step=step[1], core_step=1)

    owns = pl.pallas_call(
        functools.partial(merge_kernel, dims, slots, pos_dev),
        out_shape=[jax.ShapeDtypeStruct((packing(pos_dev)[0] * images, LANES), wire)] * pos_high,
        in_specs=[vmem] * (pos_low * z_high),
        out_specs=[vmem] * pos_high,
        scratch_shapes=[pltpu.VMEM((pos_high, pos_dev * images, LANES), jnp.float32)],
        compiler_params=pltpu.CompilerParams(vmem_limit_bytes=32 * MIB),
    )(*(got[p, z] for p in range(pos_low) for z in range(z_high)))

    near = {(0, 0): owns[0]}
    for step in far_first(pos_high, z_low):
        near[step] = send(owns[step[0]], pos_high_step=step[0], z_low_step=step[1], core_step=1)
    other = {step: send(near[step], core_step=1) for step in near}
    steps = [(0, 0), *far_first(pos_high, z_low)]
    count = max(1, len(steps) // 2)
    whole, half = steps[:count], steps[count:]
    held = jax.ShapeDtypeStruct((pos_high * z_low * CORES, pos_dev, images, LANES), jnp.float32)
    early = [block for step in whole for block in (near[step], other[step])]
    early += [near[step] for step in half]
    ready = pl.pallas_call(
        functools.partial(prepare_kernel, dims, images, pos_dev, whole, half),
        out_shape=held,
        in_specs=[vmem] * len(early),
        out_specs=vmem,
        cost_estimate=pl.CostEstimate(
            flops=0, bytes_accessed=6 * held.size, transcendentals=0
        ),
        compiler_params=pltpu.CompilerParams(vmem_limit_bytes=8 * MIB),
    )(*early)

    tall = -(-CH // ROWS) * ROWS
    mean, covariance, _ = pl.pallas_call(
        functools.partial(stats_kernel, dims, images, pos_dev, half),
        out_shape=[
            jax.ShapeDtypeStruct((pos_dev, CH), jnp.float32),
            jax.ShapeDtypeStruct((CH, pos_dev, CH), jnp.float32),
            held,
        ],
        in_specs=[vmem] * (1 + len(half)),
        out_specs=[hbm, hbm, vmem],
        input_output_aliases={0: 2},
        scratch_shapes=[
            pltpu.VMEM((pos_dev, CH), jnp.float32),
            pltpu.VMEM((pos_dev // ROWS, CH, ROWS, CH), jnp.float32),
            pltpu.VMEM((pos_dev // ROWS, tall * PITCH, LANES), jnp.float32),
            pltpu.SemaphoreType.DMA((pos_dev // ROWS + 1,)),
        ],
        compiler_params=pltpu.CompilerParams(vmem_limit_bytes=32 * MIB),
    )(ready, *(other[step] for step in half))
    return mean, jnp.transpose(covariance, (1, 0, 2))


def solution(mesh):
    in_specs = (P(("dp", "pos"), None, None), P(("dp", "pos")), P())
    out_specs = (P("pos", None), P("pos", None, None))
    return jax.shard_map(
        on_device, mesh=mesh, in_specs=in_specs, out_specs=out_specs, check_vma=False
    )
```

```python
import functools

import jax
import jax.numpy as jnp
from jax import lax
from jax.experimental import pallas as pl
from jax.experimental.pallas import tpu as pltpu
from jax.sharding import PartitionSpec as P

CH = 100
CORES = 2
LANES = 128
ROWS = 8
PITCH = ROWS + 1
MIB = 1 << 20
PIECES = 4
PIECE = CH // PIECES


def packing(pos_dev):
    extra = (pos_dev - 1) // (PIECES + 1)
    return pos_dev - extra, extra


def unpack(ref, images, pos_dev):
    block = ref[...].astype(jnp.float32)
    size = packing(pos_dev)[1] * images
    place = lax.broadcasted_iota(jnp.int32, (size, LANES), 1) // PIECE
    moved = None
    for piece in range(PIECES):
        part = pltpu.roll(block[piece * size : (piece + 1) * size], LANES - CH + piece * PIECE, 1)
        moved = part if moved is None else jnp.where(place == piece, part, moved)
    return jnp.concatenate([block, moved], axis=0).reshape(pos_dev, images, LANES)


def shift(index, n, step, sign=1):
    if n & (n - 1) == 0:
        return index ^ step
    return (index + sign * step + n) % n


def halves(n):
    small = max(f for f in range(1, n + 1) if n % f == 0 and f * f <= n)
    return small, n // small


def far_first(n_pos, n_z):
    steps = [(p, z) for p in range(n_pos) for z in range(n_z)]
    return sorted(steps, key=sum, reverse=True)[:-1]


def coordinates(dp, pos, dims):
    z_low, pos_low = dims
    z = dp // CORES
    return z // z_low, z % z_low, dp % CORES, pos // pos_low, pos % pos_low


def select_kernel(dims, pos_dev, features_hbm, counts_ref, order_hbm, *refs):
    pos_low, pos_high = dims
    *out_refs, features_ref, order_ref, picked_ref, sems = refs
    order_copy = pltpu.make_async_copy(order_hbm, order_ref, sems.at[0])
    feature_copies = [pltpu.make_async_copy(features_hbm, features_ref, sems.at[1])]
    for copy in feature_copies:
        copy.start()
    order_copy.start()
    slots, channels, positions = features_ref.shape
    x = lax.axis_index("pos") % pos_low
    lane = lax.broadcasted_iota(jnp.int32, (channels, LANES), 1)
    row = lax.broadcasted_iota(jnp.int32, (channels, LANES), 0)
    flag = lax.broadcasted_iota(jnp.int32, (positions, LANES), 1) == CH
    owned = counts_ref[0]
    order_copy.wait()
    order = order_ref[...].reshape(1, channels)[:, :LANES]
    picker = jnp.where((row == order) & (lane < CH), 1.0, 0.0).astype(jnp.bfloat16)
    for copy in feature_copies:
        copy.wait()
    for slot in range(slots):
        picked = lax.dot_general(
            features_ref[slot], picker, (((0,), (0,)), ((), ())), preferred_element_type=jnp.float32
        )
        picked = jnp.where(flag, 1.0, picked)
        picked_ref[slot] = picked * jnp.where(slot < owned, 1.0, 0.0)
    for step, out_ref in enumerate(out_refs):
        for high in range(pos_high):
            begin = (high * pos_low + shift(x, pos_low, step)) * pos_dev
            begin = pl.multiple_of(begin, pos_dev)
            for slot in range(slots):
                out_ref[pl.ds((high * slots + slot) * pos_dev, pos_dev), :] = picked_ref[
                    slot, pl.ds(begin, pos_dev), :
                ].astype(jnp.bfloat16)


def merge_kernel(dims, slots, pos_dev, *refs):
    z_low, z_high, pos_low, pos_high = dims
    in_refs, out_refs, scratch = refs[: pos_low * z_high], refs[pos_low * z_high : -1], refs[-1]
    z, _, _, y, _ = coordinates(lax.axis_index("dp"), lax.axis_index("pos"), (z_low, pos_low))
    images = len(in_refs) * slots
    size = slots * pos_dev
    for step, out_ref in enumerate(out_refs):
        begin = pl.multiple_of(shift(y, pos_high, step) * size, size)
        for source, ref in enumerate(in_refs):
            pos_step, z_step = source // z_high, source % z_high
            owner = shift(z, z_high, z_step, -1) * pos_low + pos_step
            block = ref[pl.ds(begin, size), :].astype(jnp.float32)
            for slot in range(slots):
                scratch[step, pl.ds(owner * slots + slot, pos_dev, stride=images), :] = block[
                    slot * pos_dev : (slot + 1) * pos_dev
                ]
        base, extra = packing(pos_dev)
        size_extra = extra * images
        own = lax.broadcasted_iota(jnp.int32, (size_extra, LANES), 1) < CH
        moved = scratch[step, pl.ds(base * images, size_extra), :]
        for piece in range(PIECES):
            rows = pl.ds(piece * size_extra, size_extra)
            turned = pltpu.roll(moved, CH - piece * PIECE, 1)
            out_ref[rows, :] = jnp.where(own, scratch[step, rows, :], turned).astype(jnp.bfloat16)
        rows = pl.ds(PIECES * size_extra, base * images - PIECES * size_extra)
        out_ref[rows, :] = scratch[step, rows, :].astype(jnp.bfloat16)


def places(dims, images):
    z_low, z_high, pos_low, pos_high = dims
    z_top, z, core, _, _ = coordinates(lax.axis_index("dp"), lax.axis_index("pos"), (z_low, pos_low))
    slot = lax.broadcasted_iota(jnp.int32, (1, images, LANES), 1)
    kept = slot // (images // (z_high * pos_low)) == z_top * pos_low
    where = {}
    for p in range(pos_high):
        for step in range(z_low):
            index = (shift(z, z_low, step, -1) * pos_high + p) * CORES
            near = core if p + step == 0 else 1 - core
            where[p, step] = (index + near, index + 1 - near)
    return kept, where


def put(held, kept, where, first, second):
    held[where[0]] = jnp.where(kept, first, second)
    held[where[1]] = jnp.where(kept, second, first)


def prepare_kernel(dims, images, pos_dev, whole, half, *refs):
    *in_refs, held = refs
    kept, where = places(dims, images)
    for i, step in enumerate(whole):
        first, second = (unpack(in_refs[CORES * i + j], images, pos_dev) for j in range(CORES))
        put(held, kept, where[step], first, second)
    for i, step in enumerate(half):
        held[where[step][0]] = unpack(in_refs[CORES * len(whole) + i], images, pos_dev)


def stats_kernel(dims, images, pos_dev, half, *refs):
    z_low, z_high, pos_low, pos_high = dims
    blocks = pos_high * z_low * CORES
    _, *in_refs = refs[: 1 + len(half)]
    mean_hbm, cov_hbm, held, mean_ref, cov_ref, turn_ref, sems = refs[1 + len(half) :]
    kept, where = places(dims, images)
    for step, ref in zip(half, in_refs):
        put(held, kept, where[step], held[where[step][0]], unpack(ref, images, pos_dev))
    base = packing(pos_dev)[0]
    everyone = blocks * images
    live = jnp.broadcast_to(
        held[:, base - 1].reshape(everyone, LANES)[:, CH : CH + 1], (everyone, LANES)
    )
    total = jnp.sum(live, axis=0, keepdims=True)
    root = lax.rsqrt(total - 1.0)
    weight = live * root
    tall = turn_ref.shape[1] // PITCH
    diagonal = lax.broadcasted_iota(jnp.int32, (tall, LANES), 0) == lax.broadcasted_iota(
        jnp.int32, (tall, LANES), 1
    )
    ridge = jnp.where(diagonal, 0.01, 0.0)
    groups = pos_dev // ROWS

    def out(group):
        return pltpu.make_async_copy(
            cov_ref.at[group],
            cov_hbm.at[:, pl.ds(pl.multiple_of(group * ROWS, ROWS), ROWS), :],
            sems.at[group],
        )

    def one_group(group, _):
        for row in range(ROWS):
            position = group * ROWS + row
            samples = held[:, position].reshape(everyone, LANES)
            mean = jnp.sum(samples, axis=0, keepdims=True) / total
            mean_ref[pl.ds(position, 1), :] = mean[:, :CH]
            centered = samples * root - mean * weight
            high = centered.astype(jnp.bfloat16)
            low = (centered - high.astype(jnp.float32)).astype(jnp.bfloat16)
            both = jnp.swapaxes(jnp.concatenate([high, low], axis=0), 0, 1)[:tall]
            sums = lax.dot_general(
                jnp.concatenate([both, both], axis=1),
                jnp.concatenate([high, high, low, jnp.zeros_like(low)], axis=0),
                (((1,), (0,)), ((), ())),
                preferred_element_type=jnp.float32,
            )
            turn_ref[group, pl.ds(row, tall, stride=PITCH), :] = sums + ridge
        return 0

    def finish(group):
        for channel in range(CH):
            cov_ref[group, channel] = turn_ref[group, pl.ds(channel * PITCH, ROWS), :CH]
        out(group).start()

    if everyone > 256:

        def looped(group, carry):
            one_group(group, carry)
            finish(group)
            return carry

        lax.fori_loop(0, groups, looped, 0)
    else:
        for group in range(groups):
            one_group(group, 0)
            if group:
                finish(group - 1)
        finish(groups - 1)
    mean_out = pltpu.make_async_copy(mean_ref, mean_hbm, sems.at[groups])
    mean_out.start()
    for group in range(groups):
        out(group).wait()
    mean_out.wait()


def on_device(features, counts, channel_order):
    slots, positions, channels = features.shape
    groups, dp = lax.axis_size("pos"), lax.axis_size("dp")
    depth = dp // CORES
    pos_low, pos_high = halves(groups)
    z_low, z_high = halves(depth)
    dims = (z_low, z_high, pos_low, pos_high)
    pos_dev = positions // groups
    images = pos_low * z_high * slots
    wire = jnp.bfloat16
    vmem = pl.BlockSpec(memory_space=pltpu.VMEM)
    hbm = pl.BlockSpec(memory_space=pltpu.HBM)

    def send(block, pos_low_step=0, pos_high_step=0, z_low_step=0, z_high_step=0, core_step=0):
        pairs = []
        for d in range(dp):
            for p in range(groups):
                zh, zl, core, ph, pl_ = coordinates(d, p, (z_low, pos_low))
                z = shift(zh, z_high, z_high_step) * z_low + shift(zl, z_low, z_low_step)
                q = shift(ph, pos_high, pos_high_step) * pos_low + shift(pl_, pos_low, pos_low_step)
                pairs.append((d * groups + p, (z * CORES + (core ^ core_step)) * groups + q))
        return lax.ppermute(block, ("dp", "pos"), pairs)

    half = pos_high * slots * pos_dev
    parts = pl.pallas_call(
        functools.partial(select_kernel, (pos_low, pos_high), pos_dev),
        out_shape=[jax.ShapeDtypeStruct((half, LANES), wire)] * pos_low,
        in_specs=[hbm, pl.BlockSpec(memory_space=pltpu.SMEM), hbm],
        out_specs=[vmem] * pos_low,
        scratch_shapes=[
            pltpu.VMEM((slots, channels, positions), wire),
            pltpu.VMEM((channels,), jnp.int32),
            pltpu.VMEM((slots, positions, LANES), jnp.float32),
            pltpu.SemaphoreType.DMA((1 + slots,)),
        ],
        compiler_params=pltpu.CompilerParams(vmem_limit_bytes=16 * MIB),
    )(
        pltpu.with_memory_space_constraint(jnp.transpose(features, (0, 2, 1)), pltpu.HBM),
        counts,
        pltpu.with_memory_space_constraint(channel_order, pltpu.HBM),
    )

    got = {(0, 0): parts[0]}
    for step in far_first(pos_low, z_high):
        got[step] = send(parts[step[0]], pos_low_step=step[0], z_high_step=step[1], core_step=1)

    owns = pl.pallas_call(
        functools.partial(merge_kernel, dims, slots, pos_dev),
        out_shape=[jax.ShapeDtypeStruct((packing(pos_dev)[0] * images, LANES), wire)] * pos_high,
        in_specs=[vmem] * (pos_low * z_high),
        out_specs=[vmem] * pos_high,
        scratch_shapes=[pltpu.VMEM((pos_high, pos_dev * images, LANES), jnp.float32)],
        compiler_params=pltpu.CompilerParams(vmem_limit_bytes=32 * MIB),
    )(*(got[p, z] for p in range(pos_low) for z in range(z_high)))

    near = {(0, 0): owns[0]}
    for step in far_first(pos_high, z_low):
        near[step] = send(owns[step[0]], pos_high_step=step[0], z_low_step=step[1], core_step=1)
    other = {step: send(near[step], core_step=1) for step in near}
    steps = [(0, 0), *far_first(pos_high, z_low)]
    count = max(1, len(steps) // 2)
    whole, half = steps[:count], steps[count:]
    held = jax.ShapeDtypeStruct((pos_high * z_low * CORES, pos_dev, images, LANES), jnp.float32)
    early = [block for step in whole for block in (near[step], other[step])]
    early += [near[step] for step in half]
    ready = pl.pallas_call(
        functools.partial(prepare_kernel, dims, images, pos_dev, whole, half),
        out_shape=held,
        in_specs=[vmem] * len(early),
        out_specs=vmem,
        cost_estimate=pl.CostEstimate(
            flops=0, bytes_accessed=6 * held.size, transcendentals=0
        ),
        compiler_params=pltpu.CompilerParams(vmem_limit_bytes=8 * MIB),
    )(*early)

    tall = -(-CH // ROWS) * ROWS
    mean, covariance, _ = pl.pallas_call(
        functools.partial(stats_kernel, dims, images, pos_dev, half),
        out_shape=[
            jax.ShapeDtypeStruct((pos_dev, CH), jnp.float32),
            jax.ShapeDtypeStruct((CH, pos_dev, CH), jnp.float32),
            held,
        ],
        in_specs=[vmem] * (1 + len(half)),
        out_specs=[hbm, hbm, vmem],
        input_output_aliases={0: 2},
        scratch_shapes=[
            pltpu.VMEM((pos_dev, CH), jnp.float32),
            pltpu.VMEM((pos_dev // ROWS, CH, ROWS, CH), jnp.float32),
            pltpu.VMEM((pos_dev // ROWS, tall * PITCH, LANES), jnp.float32),
            pltpu.SemaphoreType.DMA((pos_dev // ROWS + 1,)),
        ],
        compiler_params=pltpu.CompilerParams(vmem_limit_bytes=32 * MIB),
    )(ready, *(other[step] for step in half))
    return mean, jnp.transpose(covariance, (1, 0, 2))


def solution(mesh):
    in_specs = (P(("dp", "pos"), None, None), P(("dp", "pos")), P())
    out_specs = (P("pos", None), P("pos", None, None))
    return jax.shard_map(
        on_device, mesh=mesh, in_specs=in_specs, out_specs=out_specs, check_vma=False
    )
```

```python
import functools

import jax
import jax.numpy as jnp
from jax import lax
from jax.experimental import pallas as pl
from jax.experimental.pallas import tpu as pltpu
from jax.sharding import PartitionSpec as P

CH = 100
CORES = 2
LANES = 128
ROWS = 8
PITCH = ROWS + 1
MIB = 1 << 20
PIECES = 4
PIECE = CH // PIECES


def packing(pos_dev):
    extra = (pos_dev - 1) // (PIECES + 1)
    return pos_dev - extra, extra


def unpack(ref, images, pos_dev, part=0):
    base, extra = packing(pos_dev)
    block = ref[pl.ds(part * base * images, base * images), :].astype(jnp.float32)
    size = extra * images
    place = lax.broadcasted_iota(jnp.int32, (size, LANES), 1) // PIECE
    moved = None
    for piece in range(PIECES):
        turned = pltpu.roll(block[piece * size : (piece + 1) * size], LANES - CH + piece * PIECE, 1)
        moved = turned if moved is None else jnp.where(place == piece, turned, moved)
    return jnp.concatenate([block, moved], axis=0).reshape(pos_dev, images, LANES)


def shift(index, n, step, sign=1):
    if n & (n - 1) == 0:
        return index ^ step
    return (index + sign * step + n) % n


def halves(n):
    small = max(f for f in range(1, n + 1) if n % f == 0 and f * f <= n)
    return small, n // small


def far_first(n_pos, n_z):
    steps = [(p, z) for p in range(n_pos) for z in range(n_z)]
    return sorted(steps, key=sum, reverse=True)[:-1]


def coordinates(dp, pos, dims):
    z_low, pos_low = dims
    z = dp // CORES
    return z // z_low, z % z_low, dp % CORES, pos // pos_low, pos % pos_low


def select_kernel(dims, pos_dev, features_hbm, counts_ref, order_hbm, *refs):
    pos_low, pos_high = dims
    *out_refs, features_ref, order_ref, picked_ref, sems = refs
    order_copy = pltpu.make_async_copy(order_hbm, order_ref, sems.at[0])
    feature_copies = [pltpu.make_async_copy(features_hbm, features_ref, sems.at[1])]
    for copy in feature_copies:
        copy.start()
    order_copy.start()
    slots, channels, positions = features_ref.shape
    x = lax.axis_index("pos") % pos_low
    lane = lax.broadcasted_iota(jnp.int32, (channels, LANES), 1)
    row = lax.broadcasted_iota(jnp.int32, (channels, LANES), 0)
    flag = lax.broadcasted_iota(jnp.int32, (positions, LANES), 1) == CH
    owned = counts_ref[0]
    order_copy.wait()
    order = order_ref[...].reshape(1, channels)[:, :LANES]
    picker = jnp.where((row == order) & (lane < CH), 1.0, 0.0).astype(jnp.bfloat16)
    for copy in feature_copies:
        copy.wait()
    for slot in range(slots):
        picked = lax.dot_general(
            features_ref[slot], picker, (((0,), (0,)), ((), ())), preferred_element_type=jnp.float32
        )
        picked = jnp.where(flag, 1.0, picked)
        picked_ref[slot] = picked * jnp.where(slot < owned, 1.0, 0.0)
    for step, out_ref in enumerate(out_refs):
        for high in range(pos_high):
            begin = (high * pos_low + shift(x, pos_low, step)) * pos_dev
            begin = pl.multiple_of(begin, pos_dev)
            for slot in range(slots):
                out_ref[pl.ds((high * slots + slot) * pos_dev, pos_dev), :] = picked_ref[
                    slot, pl.ds(begin, pos_dev), :
                ].astype(jnp.bfloat16)


def merge_kernel(dims, slots, pos_dev, *refs):
    z_low, z_high, pos_low, pos_high = dims
    in_refs, out_refs, scratch = refs[: pos_low * z_high], refs[pos_low * z_high : -1], refs[-1]
    z, _, _, y, _ = coordinates(lax.axis_index("dp"), lax.axis_index("pos"), (z_low, pos_low))
    images = len(in_refs) * slots
    size = slots * pos_dev
    for step, out_ref in enumerate(out_refs):
        begin = pl.multiple_of(shift(y, pos_high, step) * size, size)
        for source, ref in enumerate(in_refs):
            pos_step, z_step = source // z_high, source % z_high
            owner = shift(z, z_high, z_step, -1) * pos_low + pos_step
            block = ref[pl.ds(begin, size), :].astype(jnp.float32)
            for slot in range(slots):
                scratch[step, pl.ds(owner * slots + slot, pos_dev, stride=images), :] = block[
                    slot * pos_dev : (slot + 1) * pos_dev
                ]
        base, extra = packing(pos_dev)
        size_extra = extra * images
        own = lax.broadcasted_iota(jnp.int32, (size_extra, LANES), 1) < CH
        moved = scratch[step, pl.ds(base * images, size_extra), :]
        for piece in range(PIECES):
            rows = pl.ds(piece * size_extra, size_extra)
            turned = pltpu.roll(moved, CH - piece * PIECE, 1)
            out_ref[rows, :] = jnp.where(own, scratch[step, rows, :], turned).astype(jnp.bfloat16)
        rows = pl.ds(PIECES * size_extra, base * images - PIECES * size_extra)
        out_ref[rows, :] = scratch[step, rows, :].astype(jnp.bfloat16)


def places(dims, images):
    z_low, z_high, pos_low, pos_high = dims
    z_top, z, core, _, _ = coordinates(lax.axis_index("dp"), lax.axis_index("pos"), (z_low, pos_low))
    slot = lax.broadcasted_iota(jnp.int32, (1, images, LANES), 1)
    kept = slot // (images // (z_high * pos_low)) == z_top * pos_low
    where = {}
    for p in range(pos_high):
        for step in range(z_low):
            index = (shift(z, z_low, step, -1) * pos_high + p) * CORES
            near = core if p + step == 0 else 1 - core
            where[p, step] = (index + near, index + 1 - near)
    return kept, where


def put(held, kept, where, first, second):
    held[where[0]] = jnp.where(kept, first, second)
    held[where[1]] = jnp.where(kept, second, first)


def prepare_kernel(dims, images, pos_dev, whole, half, *refs):
    *in_refs, held = refs
    kept, where = places(dims, images)
    for i, step in enumerate(whole):
        first = unpack(in_refs[i], images, pos_dev)
        put(held, kept, where[step], first, unpack(in_refs[-1], images, pos_dev, i))
    for i, step in enumerate(half):
        held[where[step][0]] = unpack(in_refs[len(whole) + i], images, pos_dev)


def stats_kernel(dims, images, pos_dev, half, *refs):
    z_low, z_high, pos_low, pos_high = dims
    blocks = pos_high * z_low * CORES
    _, in_ref, mean_hbm, cov_hbm, held, mean_ref, cov_ref, turn_ref, sems = refs
    kept, where = places(dims, images)
    for i, step in enumerate(half):
        second = unpack(in_ref, images, pos_dev, i)
        put(held, kept, where[step], held[where[step][0]], second)
    base = packing(pos_dev)[0]
    everyone = blocks * images
    live = jnp.broadcast_to(
        held[:, base - 1].reshape(everyone, LANES)[:, CH : CH + 1], (everyone, LANES)
    )
    total = jnp.sum(live, axis=0, keepdims=True)
    factor = 1.0 / (total - 1.0)
    tall = turn_ref.shape[1] // PITCH
    diagonal = lax.broadcasted_iota(jnp.int32, (tall, LANES), 0) == lax.broadcasted_iota(
        jnp.int32, (tall, LANES), 1
    )
    ridge = jnp.where(diagonal, 0.01, 0.0)
    groups = pos_dev // ROWS

    def out(group):
        return pltpu.make_async_copy(
            cov_ref.at[group],
            cov_hbm.at[:, pl.ds(pl.multiple_of(group * ROWS, ROWS), ROWS), :],
            sems.at[group],
        )

    def one_group(group, _):
        for row in range(ROWS):
            position = group * ROWS + row
            samples = held[:, position].reshape(everyone, LANES)
            mean = jnp.sum(samples, axis=0, keepdims=True) / total
            mean_ref[pl.ds(position, 1), :] = mean[:, :CH]
            centered = samples - mean * live
            high = centered.astype(jnp.bfloat16)
            low = (centered - high.astype(jnp.float32)).astype(jnp.bfloat16)
            both = jnp.swapaxes(jnp.concatenate([high, low], axis=0), 0, 1)[:tall]
            sums = lax.dot_general(
                jnp.concatenate([both, both], axis=1),
                jnp.concatenate([high, high, low, jnp.zeros_like(low)], axis=0),
                (((1,), (0,)), ((), ())),
                preferred_element_type=jnp.float32,
            )
            turn_ref[group, pl.ds(row, tall, stride=PITCH), :] = sums * factor + ridge
        for channel in range(CH):
            cov_ref[group, channel] = turn_ref[group, pl.ds(channel * PITCH, ROWS), :CH]
        out(group).start()
        return 0

    if everyone > 256:
        lax.fori_loop(0, groups, one_group, 0)
    else:
        for group in range(groups):
            one_group(group, 0)
    mean_out = pltpu.make_async_copy(mean_ref, mean_hbm, sems.at[groups])
    mean_out.start()
    for group in range(groups):
        out(group).wait()
    mean_out.wait()


def on_device(features, counts, channel_order):
    slots, positions, channels = features.shape
    groups, dp = lax.axis_size("pos"), lax.axis_size("dp")
    depth = dp // CORES
    pos_low, pos_high = halves(groups)
    z_low, z_high = halves(depth)
    dims = (z_low, z_high, pos_low, pos_high)
    pos_dev = positions // groups
    images = pos_low * z_high * slots
    wire = jnp.bfloat16
    vmem = pl.BlockSpec(memory_space=pltpu.VMEM)
    hbm = pl.BlockSpec(memory_space=pltpu.HBM)

    def send(block, pos_low_step=0, pos_high_step=0, z_low_step=0, z_high_step=0, core_step=0):
        pairs = []
        for d in range(dp):
            for p in range(groups):
                zh, zl, core, ph, pl_ = coordinates(d, p, (z_low, pos_low))
                z = shift(zh, z_high, z_high_step) * z_low + shift(zl, z_low, z_low_step)
                q = shift(ph, pos_high, pos_high_step) * pos_low + shift(pl_, pos_low, pos_low_step)
                pairs.append((d * groups + p, (z * CORES + (core ^ core_step)) * groups + q))
        return lax.ppermute(block, ("dp", "pos"), pairs)

    half = pos_high * slots * pos_dev
    parts = pl.pallas_call(
        functools.partial(select_kernel, (pos_low, pos_high), pos_dev),
        out_shape=[jax.ShapeDtypeStruct((half, LANES), wire)] * pos_low,
        in_specs=[hbm, pl.BlockSpec(memory_space=pltpu.SMEM), hbm],
        out_specs=[vmem] * pos_low,
        scratch_shapes=[
            pltpu.VMEM((slots, channels, positions), wire),
            pltpu.VMEM((channels,), jnp.int32),
            pltpu.VMEM((slots, positions, LANES), jnp.float32),
            pltpu.SemaphoreType.DMA((1 + slots,)),
        ],
        compiler_params=pltpu.CompilerParams(vmem_limit_bytes=16 * MIB),
    )(
        pltpu.with_memory_space_constraint(jnp.transpose(features, (0, 2, 1)), pltpu.HBM),
        counts,
        pltpu.with_memory_space_constraint(channel_order, pltpu.HBM),
    )

    got = {(0, 0): parts[0]}
    for step in far_first(pos_low, z_high):
        got[step] = send(parts[step[0]], pos_low_step=step[0], z_high_step=step[1], core_step=1)

    owns = pl.pallas_call(
        functools.partial(merge_kernel, dims, slots, pos_dev),
        out_shape=[jax.ShapeDtypeStruct((packing(pos_dev)[0] * images, LANES), wire)] * pos_high,
        in_specs=[vmem] * (pos_low * z_high),
        out_specs=[vmem] * pos_high,
        scratch_shapes=[pltpu.VMEM((pos_high, pos_dev * images, LANES), jnp.float32)],
        compiler_params=pltpu.CompilerParams(vmem_limit_bytes=32 * MIB),
    )(*(got[p, z] for p in range(pos_low) for z in range(z_high)))

    near = {(0, 0): owns[0]}
    for step in far_first(pos_high, z_low):
        near[step] = send(owns[step[0]], pos_high_step=step[0], z_low_step=step[1], core_step=1)
    steps = [(0, 0), *far_first(pos_high, z_low)]
    count = max(1, len(steps) // 2)
    whole, half = steps[:count], steps[count:]
    early_other = send(jnp.concatenate([near[step] for step in whole], axis=0), core_step=1)
    late = send(jnp.concatenate([near[step] for step in half], axis=0), core_step=1)
    held = jax.ShapeDtypeStruct((pos_high * z_low * CORES, pos_dev, images, LANES), jnp.float32)
    early = [near[step] for step in (*whole, *half)] + [early_other]
    ready = pl.pallas_call(
        functools.partial(prepare_kernel, dims, images, pos_dev, whole, half),
        out_shape=held,
        in_specs=[vmem] * len(early),
        out_specs=vmem,
        cost_estimate=pl.CostEstimate(
            flops=0, bytes_accessed=6 * held.size, transcendentals=0
        ),
        compiler_params=pltpu.CompilerParams(vmem_limit_bytes=8 * MIB),
    )(*early)

    tall = -(-CH // ROWS) * ROWS
    mean, covariance, _ = pl.pallas_call(
        functools.partial(stats_kernel, dims, images, pos_dev, half),
        out_shape=[
            jax.ShapeDtypeStruct((pos_dev, CH), jnp.float32),
            jax.ShapeDtypeStruct((CH, pos_dev, CH), jnp.float32),
            held,
        ],
        in_specs=[vmem, vmem],
        out_specs=[hbm, hbm, vmem],
        input_output_aliases={0: 2},
        scratch_shapes=[
            pltpu.VMEM((pos_dev, CH), jnp.float32),
            pltpu.VMEM((pos_dev // ROWS, CH, ROWS, CH), jnp.float32),
            pltpu.VMEM((pos_dev // ROWS, tall * PITCH, LANES), jnp.float32),
            pltpu.SemaphoreType.DMA((pos_dev // ROWS + 1,)),
        ],
        compiler_params=pltpu.CompilerParams(vmem_limit_bytes=32 * MIB),
    )(ready, late)
    return mean, jnp.transpose(covariance, (1, 0, 2))


def solution(mesh):
    in_specs = (P(("dp", "pos"), None, None), P(("dp", "pos")), P())
    out_specs = (P("pos", None), P("pos", None, None))
    return jax.shard_map(
        on_device, mesh=mesh, in_specs=in_specs, out_specs=out_specs, check_vma=False
    )
```

```python
import functools

import jax
import jax.numpy as jnp
from jax import lax
from jax.experimental import pallas as pl
from jax.experimental.pallas import tpu as pltpu
from jax.sharding import PartitionSpec as P

CH = 100
CORES = 2
LANES = 128
ROWS = 8
PITCH = ROWS + 1
MIB = 1 << 20
PIECES = 4
PIECE = CH // PIECES


def packing(pos_dev):
    extra = (pos_dev - 1) // (PIECES + 1)
    return pos_dev - extra, extra


def unpack(ref, images, pos_dev):
    block = ref[...].astype(jnp.float32)
    size = packing(pos_dev)[1] * images
    place = lax.broadcasted_iota(jnp.int32, (size, LANES), 1) // PIECE
    moved = None
    for piece in range(PIECES):
        part = pltpu.roll(block[piece * size : (piece + 1) * size], LANES - CH + piece * PIECE, 1)
        moved = part if moved is None else jnp.where(place == piece, part, moved)
    return jnp.concatenate([block, moved], axis=0).reshape(pos_dev, images, LANES)


def shift(index, n, step, sign=1):
    if n & (n - 1) == 0:
        return index ^ step
    return (index + sign * step + n) % n


def halves(n):
    small = max(f for f in range(1, n + 1) if n % f == 0 and f * f <= n)
    return small, n // small


def far_first(n_pos, n_z):
    steps = [(p, z) for p in range(n_pos) for z in range(n_z)]
    return sorted(steps, key=sum, reverse=True)[:-1]


def coordinates(dp, pos, dims):
    z_low, pos_low = dims
    z = dp // CORES
    return z // z_low, z % z_low, dp % CORES, pos // pos_low, pos % pos_low


def select_kernel(dims, pos_dev, features_hbm, counts_ref, order_hbm, *refs):
    pos_low, pos_high = dims
    *out_refs, features_ref, order_ref, picked_ref, sems = refs
    order_copy = pltpu.make_async_copy(order_hbm, order_ref, sems.at[0])
    feature_copies = [pltpu.make_async_copy(features_hbm, features_ref, sems.at[1])]
    for copy in feature_copies:
        copy.start()
    order_copy.start()
    slots, channels, positions = features_ref.shape
    x = lax.axis_index("pos") % pos_low
    lane = lax.broadcasted_iota(jnp.int32, (channels, LANES), 1)
    row = lax.broadcasted_iota(jnp.int32, (channels, LANES), 0)
    flag = lax.broadcasted_iota(jnp.int32, (positions, LANES), 1) == CH
    owned = counts_ref[0]
    order_copy.wait()
    order = order_ref[...].reshape(1, channels)[:, :LANES]
    picker = jnp.where((row == order) & (lane < CH), 1.0, 0.0).astype(jnp.bfloat16)
    for copy in feature_copies:
        copy.wait()
    for slot in range(slots):
        picked = lax.dot_general(
            features_ref[slot], picker, (((0,), (0,)), ((), ())), preferred_element_type=jnp.float32
        )
        picked = jnp.where(flag, 1.0, picked)
        picked_ref[slot] = picked * jnp.where(slot < owned, 1.0, 0.0)
    for step, out_ref in enumerate(out_refs):
        for high in range(pos_high):
            begin = (high * pos_low + shift(x, pos_low, step)) * pos_dev
            begin = pl.multiple_of(begin, pos_dev)
            for slot in range(slots):
                out_ref[pl.ds((high * slots + slot) * pos_dev, pos_dev), :] = picked_ref[
                    slot, pl.ds(begin, pos_dev), :
                ].astype(jnp.bfloat16)


def merge_kernel(dims, slots, pos_dev, *refs):
    z_low, z_high, pos_low, pos_high = dims
    in_refs, out_refs, scratch = refs[: pos_low * z_high], refs[pos_low * z_high : -1], refs[-1]
    z, _, _, y, _ = coordinates(lax.axis_index("dp"), lax.axis_index("pos"), (z_low, pos_low))
    images = len(in_refs) * slots
    size = slots * pos_dev
    for step, out_ref in enumerate(out_refs):
        begin = pl.multiple_of(shift(y, pos_high, step) * size, size)
        for source, ref in enumerate(in_refs):
            pos_step, z_step = source // z_high, source % z_high
            owner = shift(z, z_high, z_step, -1) * pos_low + pos_step
            block = ref[pl.ds(begin, size), :].astype(jnp.float32)
            for slot in range(slots):
                scratch[step, pl.ds(owner * slots + slot, pos_dev, stride=images), :] = block[
                    slot * pos_dev : (slot + 1) * pos_dev
                ]
        base, extra = packing(pos_dev)
        size_extra = extra * images
        own = lax.broadcasted_iota(jnp.int32, (size_extra, LANES), 1) < CH
        moved = scratch[step, pl.ds(base * images, size_extra), :]
        for piece in range(PIECES):
            rows = pl.ds(piece * size_extra, size_extra)
            turned = pltpu.roll(moved, CH - piece * PIECE, 1)
            out_ref[rows, :] = jnp.where(own, scratch[step, rows, :], turned).astype(jnp.bfloat16)
        rows = pl.ds(PIECES * size_extra, base * images - PIECES * size_extra)
        out_ref[rows, :] = scratch[step, rows, :].astype(jnp.bfloat16)


def places(dims, images):
    z_low, z_high, pos_low, pos_high = dims
    z_top, z, core, _, _ = coordinates(lax.axis_index("dp"), lax.axis_index("pos"), (z_low, pos_low))
    slot = lax.broadcasted_iota(jnp.int32, (1, images, LANES), 1)
    kept = slot // (images // (z_high * pos_low)) == z_top * pos_low
    where = {}
    for p in range(pos_high):
        for step in range(z_low):
            index = (shift(z, z_low, step, -1) * pos_high + p) * CORES
            near = core if p + step == 0 else 1 - core
            where[p, step] = (index + near, index + 1 - near)
    return kept, where


def put(held, kept, where, first, second):
    held[where[0]] = jnp.where(kept, first, second)
    held[where[1]] = jnp.where(kept, second, first)


def prepare_kernel(dims, images, pos_dev, whole, half, *refs):
    *in_refs, held = refs
    kept, where = places(dims, images)
    for i, step in enumerate(whole):
        first, second = (unpack(in_refs[CORES * i + j], images, pos_dev) for j in range(CORES))
        put(held, kept, where[step], first, second)
    for i, step in enumerate(half):
        held[where[step][0]] = unpack(in_refs[CORES * len(whole) + i], images, pos_dev)


def stats_kernel(dims, images, pos_dev, half, *refs):
    z_low, z_high, pos_low, pos_high = dims
    blocks = pos_high * z_low * CORES
    _, *in_refs = refs[: 1 + len(half)]
    mean_hbm, cov_hbm, held, mean_ref, cov_ref, turn_ref, sems = refs[1 + len(half) :]
    kept, where = places(dims, images)
    for step, ref in zip(half, in_refs):
        put(held, kept, where[step], held[where[step][0]], unpack(ref, images, pos_dev))
    base = packing(pos_dev)[0]
    everyone = blocks * images
    live = jnp.broadcast_to(
        held[:, base - 1].reshape(everyone, LANES)[:, CH : CH + 1], (everyone, LANES)
    )
    total = jnp.sum(live, axis=0, keepdims=True)
    factor = 1.0 / (total - 1.0)
    tall = turn_ref.shape[1] // PITCH
    diagonal = lax.broadcasted_iota(jnp.int32, (tall, LANES), 0) == lax.broadcasted_iota(
        jnp.int32, (tall, LANES), 1
    )
    ridge = jnp.where(diagonal, 0.01, 0.0)
    groups = pos_dev // ROWS

    def out(group):
        return pltpu.make_async_copy(
            cov_ref.at[group],
            cov_hbm.at[:, pl.ds(pl.multiple_of(group * ROWS, ROWS), ROWS), :],
            sems.at[group],
        )

    def one_group(group, _):
        tiles = []
        for row in range(ROWS):
            position = group * ROWS + row
            samples = held[:, position].reshape(everyone, LANES)
            mean = jnp.sum(samples, axis=0, keepdims=True) / total
            mean_ref[pl.ds(position, 1), :] = mean[:, :CH]
            centered = samples - mean * live
            high = centered.astype(jnp.bfloat16)
            low = (centered - high.astype(jnp.float32)).astype(jnp.bfloat16)
            both = jnp.swapaxes(jnp.concatenate([high, low], axis=0), 0, 1)[:tall]
            sums = lax.dot_general(
                jnp.concatenate([both, both], axis=1),
                jnp.concatenate([high, high, low, jnp.zeros_like(low)], axis=0),
                (((1,), (0,)), ((), ())),
                preferred_element_type=jnp.float32,
            )
            tiles.append(sums * factor + ridge)
        cov_ref[group] = jnp.swapaxes(jnp.stack(tiles), 0, 1)[:CH, :, :CH]
        out(group).start()
        return 0

    if everyone > 256:
        lax.fori_loop(0, groups, one_group, 0)
    else:
        for group in range(groups):
            one_group(group, 0)
    mean_out = pltpu.make_async_copy(mean_ref, mean_hbm, sems.at[groups])
    mean_out.start()
    for group in range(groups):
        out(group).wait()
    mean_out.wait()


def on_device(features, counts, channel_order):
    slots, positions, channels = features.shape
    groups, dp = lax.axis_size("pos"), lax.axis_size("dp")
    depth = dp // CORES
    pos_low, pos_high = halves(groups)
    z_low, z_high = halves(depth)
    dims = (z_low, z_high, pos_low, pos_high)
    pos_dev = positions // groups
    images = pos_low * z_high * slots
    wire = jnp.bfloat16
    vmem = pl.BlockSpec(memory_space=pltpu.VMEM)
    hbm = pl.BlockSpec(memory_space=pltpu.HBM)

    def send(block, pos_low_step=0, pos_high_step=0, z_low_step=0, z_high_step=0, core_step=0):
        pairs = []
        for d in range(dp):
            for p in range(groups):
                zh, zl, core, ph, pl_ = coordinates(d, p, (z_low, pos_low))
                z = shift(zh, z_high, z_high_step) * z_low + shift(zl, z_low, z_low_step)
                q = shift(ph, pos_high, pos_high_step) * pos_low + shift(pl_, pos_low, pos_low_step)
                pairs.append((d * groups + p, (z * CORES + (core ^ core_step)) * groups + q))
        return lax.ppermute(block, ("dp", "pos"), pairs)

    half = pos_high * slots * pos_dev
    parts = pl.pallas_call(
        functools.partial(select_kernel, (pos_low, pos_high), pos_dev),
        out_shape=[jax.ShapeDtypeStruct((half, LANES), wire)] * pos_low,
        in_specs=[hbm, pl.BlockSpec(memory_space=pltpu.SMEM), hbm],
        out_specs=[vmem] * pos_low,
        scratch_shapes=[
            pltpu.VMEM((slots, channels, positions), wire),
            pltpu.VMEM((channels,), jnp.int32),
            pltpu.VMEM((slots, positions, LANES), jnp.float32),
            pltpu.SemaphoreType.DMA((1 + slots,)),
        ],
        compiler_params=pltpu.CompilerParams(vmem_limit_bytes=16 * MIB),
    )(
        pltpu.with_memory_space_constraint(jnp.transpose(features, (0, 2, 1)), pltpu.HBM),
        counts,
        pltpu.with_memory_space_constraint(channel_order, pltpu.HBM),
    )

    got = {(0, 0): parts[0]}
    for step in far_first(pos_low, z_high):
        got[step] = send(parts[step[0]], pos_low_step=step[0], z_high_step=step[1], core_step=1)

    owns = pl.pallas_call(
        functools.partial(merge_kernel, dims, slots, pos_dev),
        out_shape=[jax.ShapeDtypeStruct((packing(pos_dev)[0] * images, LANES), wire)] * pos_high,
        in_specs=[vmem] * (pos_low * z_high),
        out_specs=[vmem] * pos_high,
        scratch_shapes=[pltpu.VMEM((pos_high, pos_dev * images, LANES), jnp.float32)],
        compiler_params=pltpu.CompilerParams(vmem_limit_bytes=32 * MIB),
    )(*(got[p, z] for p in range(pos_low) for z in range(z_high)))

    near = {(0, 0): owns[0]}
    for step in far_first(pos_high, z_low):
        near[step] = send(owns[step[0]], pos_high_step=step[0], z_low_step=step[1], core_step=1)
    other = {step: send(near[step], core_step=1) for step in near}
    steps = [(0, 0), *far_first(pos_high, z_low)]
    count = max(1, len(steps) // 2)
    whole, half = steps[:count], steps[count:]
    held = jax.ShapeDtypeStruct((pos_high * z_low * CORES, pos_dev, images, LANES), jnp.float32)
    early = [block for step in whole for block in (near[step], other[step])]
    early += [near[step] for step in half]
    ready = pl.pallas_call(
        functools.partial(prepare_kernel, dims, images, pos_dev, whole, half),
        out_shape=held,
        in_specs=[vmem] * len(early),
        out_specs=vmem,
        cost_estimate=pl.CostEstimate(
            flops=0, bytes_accessed=6 * held.size, transcendentals=0
        ),
        compiler_params=pltpu.CompilerParams(vmem_limit_bytes=8 * MIB),
    )(*early)

    tall = -(-CH // ROWS) * ROWS
    mean, covariance, _ = pl.pallas_call(
        functools.partial(stats_kernel, dims, images, pos_dev, half),
        out_shape=[
            jax.ShapeDtypeStruct((pos_dev, CH), jnp.float32),
            jax.ShapeDtypeStruct((CH, pos_dev, CH), jnp.float32),
            held,
        ],
        in_specs=[vmem] * (1 + len(half)),
        out_specs=[hbm, hbm, vmem],
        input_output_aliases={0: 2},
        scratch_shapes=[
            pltpu.VMEM((pos_dev, CH), jnp.float32),
            pltpu.VMEM((pos_dev // ROWS, CH, ROWS, CH), jnp.float32),
            pltpu.VMEM((pos_dev // ROWS, tall * PITCH, LANES), jnp.float32),
            pltpu.SemaphoreType.DMA((pos_dev // ROWS + 1,)),
        ],
        compiler_params=pltpu.CompilerParams(vmem_limit_bytes=32 * MIB),
    )(ready, *(other[step] for step in half))
    return mean, jnp.transpose(covariance, (1, 0, 2))


def solution(mesh):
    in_specs = (P(("dp", "pos"), None, None), P(("dp", "pos")), P())
    out_specs = (P("pos", None), P("pos", None, None))
    return jax.shard_map(
        on_device, mesh=mesh, in_specs=in_specs, out_specs=out_specs, check_vma=False
    )
```
